256 devices in a mesh: tok: 32 (over y, x, core), mlp: 8 (over z).
Axes of the slice: x: 4, y: 4, z: 8, core: 2. Of those that a mesh axis runs over, the one named last changes fastest.
Arguments:
- states: bfloat16 [8, 512, 2048], P(None, 'tok', 'mlp')
- w_qkv: bfloat16 [2048, 6144], P('tok', 'mlp')
- w_out: bfloat16 [2048, 2048], P('mlp', 'tok'), may hold values from -0.25 to 0.25
- w_up: bfloat16 [2048, 8192], P(None, 'mlp'), may hold values from -0.125 to 0.125
- w_down: bfloat16 [8192, 2048], P('mlp'), may hold values from -0.0625 to 0.0625
- w_dec: bfloat16 [2048, 128], P('mlp'), may hold values from -0.125 to 0.125
- gain_attn: float32 [2048], replicated, may hold values from 0.25 to 1.75
- gain_mlp: float32 [2048], P('mlp'), may hold values from 0.25 to 1.75
- obs_patch: int32 [256, 32, 64], P(('tok', 'mlp')), may hold values from 0 to 127
- obs_base: int32 [256, 32, 64], P(('tok', 'mlp')), may hold values from 0 to 110, as said below
- obs_count: int32 [256, 32], P(('tok', 'mlp')), may hold values from 1 to 64, as said below
- obs_weight: float32 [256, 32, 4, 64], P(('tok', 'mlp')), may hold values from 0.1 to 1
- obs_value: float32 [256, 32, 64], P(('tok', 'mlp')), may hold values from -6 to 6
Outputs:
- state_out: bfloat16 [8, 512, 2048], P(None, 'tok', 'mlp')
- guidance: float32 [8, 512, 2048], P(None, 'tok', 'mlp')
The draws below stay inside these ranges and needn't reach their ends.
Inputs may be any that keep to these rules, and one draw needn't show every extreme that they name: `obs_base`: base = r * 16 + c with r below 7 and c below 15. `obs_count`: slots at or above the count are padding; every source device has one block with all 64 slots live.
All inputs are finite; a program needn't handle non-finite values.
Results may differ from the reference program's by a relative error of at most 0.028.
Values may be sent and summed in bfloat16 or wider, within the bound.
No kernel may reach another device: no remote copies, remote signals or barrier semaphores. Data moves between devices by JAX's collectives and lax.ppermute only.
A program may use at most 128 MiB of HBM per device.

```python
import jax
import jax.numpy as jnp
from jax import lax

D = 2048
HEADS = 32
HD = 64
FF = 8192
LEN = 512
CAP = 64
PROWS = 8
PW = 16
PV = 128
SEQS = 8
ROWS = 128
N_TOK = 32
N_MLP = 8


def draw_states(key, part):
    key = jax.random.fold_in(key, 11)
    keys = jax.random.split(key, 3)
    base = jax.random.normal(keys[0], (SEQS, LEN, D), jnp.float32)
    rise = 1.2528
    row_scale = jnp.exp(jax.random.uniform(keys[1], (SEQS, LEN, 1), jnp.float32, 0.0, 2.3026))
    column = jnp.arange(D, dtype=jnp.float32) / (D - 1)
    jitter = jax.random.uniform(keys[2], (D,), jnp.float32, -0.2, 0.2)
    col_scale = jnp.exp(rise * column + jitter).reshape(1, 1, D)
    return (base * row_scale * col_scale * 0.03).astype(jnp.bfloat16)


def draw_w_qkv(key, part):
    key = jax.random.fold_in(key, 23)
    keys = jax.random.split(key, 3)
    groups = HEADS // N_MLP
    shape = (D, N_MLP, 1, groups, HD)
    query = jax.random.normal(keys[0], shape, jnp.float32)
    noise = jax.random.normal(keys[1], shape, jnp.float32)
    values = jax.random.normal(keys[2], shape, jnp.float32)
    keys_part = noise
    stacked = jnp.concatenate([query, keys_part, values], axis=2)
    return (stacked * D ** (-0.5)).reshape(D, 3 * D).astype(jnp.bfloat16)


def draw_obs_base(key, part):
    key = jax.random.fold_in(key, 37)
    keys = jax.random.split(key, 2)
    shape = (N_TOK * N_MLP, N_TOK, CAP)
    row = jax.random.randint(keys[0], shape, 0, PROWS - 1)
    col = jax.random.randint(keys[1], shape, 0, PW - 1)
    return (row * PW + col).astype(jnp.int32)


def draw_obs_count(key, part):
    key = jax.random.fold_in(key, 41)
    keys = jax.random.split(key, 3)
    sources = N_TOK * N_MLP
    low = jax.random.randint(keys[0], (1, N_TOK), 1, CAP + 1)
    counts = jax.random.randint(keys[1], (sources, N_TOK), low, CAP + 1)
    full = jax.random.randint(keys[2], (sources, 1), 0, N_TOK)
    column = jnp.arange(N_TOK, dtype=jnp.int32)[None, :]
    return jnp.where(column == full, CAP, counts).astype(jnp.int32)


def touch_ends(drawn, rng, smallest, high):
    longest = drawn.shape.index(max(drawn.shape))
    spots = []
    for shift in (0, 1):
        where = [jax.random.randint(jax.random.fold_in(rng, axis), (), 0, length) for axis, length in enumerate(drawn.shape)]
        where[longest] = (where[longest] + shift) % drawn.shape[longest]
        spots.append(tuple(where))
    return drawn.at[spots[0]].set(smallest).at[spots[1]].set(high)


def block_scale(rng, extent, cuts, least, largest):
    level, own = 1.0, jax.random.fold_in(rng, 6)
    for position, shards_of in cuts:
        heights = jnp.exp(jax.random.uniform(jax.random.fold_in(own, position), (shards_of,), jnp.float32, least / len(cuts), largest / len(cuts)))
        level = level * jnp.repeat(heights, extent[position] // shards_of).reshape([-1 if axis == position else 1 for axis in range(len(extent))])
    return level


def gaussian(key, dims, deviation, limit, cuts=(), kind=jnp.bfloat16):
    loudness = block_scale(key, dims, cuts, -0.22, 0.18) if cuts else 1.0
    values = jax.random.normal(key, dims, jnp.float32) * deviation * loudness
    return jnp.minimum(jnp.maximum(values, -limit), limit).astype(kind)


def setup_inputs(seed: int = 0) -> dict:
    splits = jax.random.split(jax.random.key(seed), 14)
    return {
        "states": draw_states(jax.random.fold_in(splits[13], 71), 0),
        "w_qkv": draw_w_qkv(jax.random.fold_in(splits[13], 71), 0),
        "w_out": gaussian(splits[2], (D, D), (D // 4) ** -0.5, 0.25, ((0, 8), (1, 32))),
        "w_up": gaussian(splits[3], (D, FF), D ** -0.5, 0.125, ((1, 8),)),
        "w_down": gaussian(splits[4], (FF, D), FF ** -0.5, 0.0625, ((0, 8),)),
        "w_dec": gaussian(splits[5], (D, PV), D ** -0.5, 0.125, ((0, 8),)),
        "gain_attn": jnp.clip(1.0 + 0.15 * jax.random.normal(splits[6], (D,), jnp.float32), 0.25, 1.75),
        "gain_mlp": jnp.clip(1.0 + 0.15 * jax.random.normal(splits[7], (D,), jnp.float32), 0.25, 1.75),
        "obs_patch": touch_ends(jax.random.randint(splits[8], (N_TOK * N_MLP, N_TOK, CAP), 0, ROWS), jax.random.fold_in(splits[8], 1), 0, ROWS - 1).astype(jnp.int32),
        "obs_base": draw_obs_base(jax.random.fold_in(splits[13], 71), 0),
        "obs_count": draw_obs_count(jax.random.fold_in(splits[13], 71), 0),
        "obs_weight": jnp.clip(0.1 + 0.9 * jax.random.uniform(splits[11], (N_TOK * N_MLP, N_TOK, 4, CAP), jnp.float32) ** block_scale(splits[11], (N_TOK * N_MLP, N_TOK, 4, CAP), ((0, 256),), -0.2, 0.2), 0.1, 1.0),
        "obs_value": gaussian(splits[12], (N_TOK * N_MLP, N_TOK, CAP), 1.0, 6.0, ((0, 256),), jnp.float32),
    }


EPS = 1e-06

def attend_pair(triple):
    query, keys, values = triple
    length = query.shape[0]
    block = min(512, length)
    scale = 1.0 / HD ** 0.5

    def one_block(rows):
        scores = jnp.dot(rows, keys.T, preferred_element_type=jnp.float32) * scale
        top = lax.optimization_barrier(jnp.max(scores, axis=1, keepdims=True))
        probs = jnp.exp(scores - top)
        total = lax.optimization_barrier(jnp.sum(probs, axis=1, keepdims=True))
        mixed = jnp.dot(probs.astype(jnp.bfloat16), values, preferred_element_type=jnp.float32)
        return (mixed / total).astype(jnp.bfloat16)
    blocks = lax.map(one_block, query.reshape(length // block, block, HD))
    return blocks.reshape(length, HD)

def rounded(term):
    low = lax.optimization_barrier(term.astype(jnp.bfloat16))
    return low.astype(jnp.float32)

def reference(states, w_qkv, w_out, w_up, w_down, w_dec, gain_attn, gain_mlp, obs_patch, obs_base, obs_count, obs_weight, obs_value):
    tokens = SEQS * LEN
    groups = HEADS // N_MLP
    width = groups * HD
    flat = states.reshape(tokens, D).astype(jnp.float32)
    normed = (flat * lax.rsqrt(lax.optimization_barrier(jnp.mean(flat * flat, axis=1, keepdims=True)) + EPS) * gain_attn).astype(jnp.bfloat16)
    qkv = jnp.dot(normed, w_qkv, preferred_element_type=jnp.float32).astype(jnp.bfloat16)
    qkv = qkv.reshape(SEQS, LEN, N_MLP, 3, groups, HD)

    def heads_of(part):
        picked = qkv[:, :, :, part].reshape(SEQS, LEN, HEADS, HD)
        return picked.transpose(0, 2, 1, 3).reshape(SEQS * HEADS, LEN, HD)
    attended = lax.map(attend_pair, (heads_of(0), heads_of(1), heads_of(2)))
    attended = attended.reshape(SEQS, HEADS, LEN, HD).transpose(0, 2, 1, 3).reshape(tokens, D)
    attn = jnp.zeros((tokens, D), jnp.float32)
    for group in range(N_MLP):
        cols = attended[:, group * width:(group + 1) * width]
        attn = attn + rounded(jnp.dot(cols, w_out[group * width:(group + 1) * width], preferred_element_type=jnp.float32))
    resid = flat + attn
    normed2 = (resid * lax.rsqrt(lax.optimization_barrier(jnp.mean(resid * resid, axis=1, keepdims=True)) + EPS) * gain_mlp).astype(jnp.bfloat16)
    hidden = jax.nn.gelu(jnp.dot(normed2, w_up, preferred_element_type=jnp.float32)).astype(jnp.bfloat16)
    share = FF // N_MLP
    ffn = jnp.zeros((tokens, D), jnp.float32)
    for group in range(N_MLP):
        cols = hidden[:, group * share:(group + 1) * share]
        ffn = ffn + rounded(jnp.dot(cols, w_down[group * share:(group + 1) * share], preferred_element_type=jnp.float32))
    state_out = (resid + ffn).astype(jnp.bfloat16)
    decoded = jnp.dot(state_out, w_dec, preferred_element_type=jnp.float32)
    pos = LEN // N_TOK
    dest = jnp.arange(N_TOK, dtype=jnp.int32)[None, :, None]
    token = obs_patch // pos * LEN + dest * pos + obs_patch % pos
    start = token * PV + obs_base
    offsets = jnp.array([0, 1, PW, PW + 1], dtype=jnp.int32)
    taps = start[:, :, None, :] + offsets[None, None, :, None]
    flat_dec = decoded.reshape(-1)
    interp = lax.optimization_barrier(jnp.sum(obs_weight * flat_dec[taps], axis=2))
    live = jnp.arange(CAP, dtype=jnp.int32)[None, None, :] < obs_count[:, :, None]
    misfit = jnp.where(live, interp - obs_value, 0.0)
    contrib = obs_weight * misfit[:, :, None, :]
    grad_dec = jnp.zeros((tokens * PV,), jnp.float32).at[taps.reshape(-1)].add(contrib.reshape(-1))
    guidance = jnp.dot(grad_dec.reshape(tokens, PV), w_dec.astype(jnp.float32).T, precision=lax.Precision.HIGHEST)
    return (state_out.reshape(SEQS, LEN, D), guidance.reshape(SEQS, LEN, D))
```

```python
import functools

import jax
import jax.numpy as jnp
from jax import lax
from jax.experimental import pallas as pl
from jax.experimental.pallas import tpu as pltpu
from jax.sharding import PartitionSpec as P

D = 2048
HD = 64
EPS = 1e-06
BF = jnp.bfloat16
F32 = jnp.float32
NT = (((1,), (1,)), ((), ()))
GELU = 0.7978845608028654
STEPS = (0, 1, 15, 16, 17)


def params(mib):
    return pltpu.CompilerParams(vmem_limit_bytes=mib * 1024 * 1024)


def lanes(shape):
    return lax.broadcasted_iota(jnp.int32, shape, len(shape) - 1)


def half(x):
    return pltpu.roll(x, 64, 1)


def left(shape):
    return lanes(shape) < 64


def pack_kernel(wqkv, wout_t, obs, out):
    n = out.shape[0]
    for dest in range(n):
        c = dest % 2
        for j in range(3):
            out[dest, 64 * j : 64 * j + 64, :] = wqkv[:, 256 * j + 128 * c : 256 * j + 128 * c + 128]
        out[dest, 192:256, :] = wout_t[:, 128 * c : 128 * c + 128]
    out[:, 256:272, :] = obs[...]


def norm_kernel(me, *refs):
    packs, sib, gain = refs[:8], refs[8], refs[9]
    normed, wdec, ginv = refs[10:]
    m = me[0]
    own_sq = jnp.zeros((128, 1), F32)
    sib_sq = jnp.zeros((128, 1), F32)
    for d in range(8):
        a = packs[d][0:128, :].astype(F32)
        b = sib[d].astype(F32)
        own_sq += jnp.sum(a * a, axis=1, keepdims=True)
        sib_sq += jnp.sum(b * b, axis=1, keepdims=True)
    own_r = lax.rsqrt(own_sq / D + EPS)
    sib_r = lax.rsqrt(sib_sq / D + EPS)
    for d in range(8):
        at = lax.rem(m - d + 8, 8)
        g = gain[at]
        normed[at, 0:128, :] = (packs[d][0:128, :].astype(F32) * own_r * g).astype(BF)
        normed[at, 128:256, :] = (sib[d].astype(F32) * sib_r * g).astype(BF)
        wdec[at, 0:128, :] = packs[d][144:272, 0:128]
        wdec[at, 128:256, :] = packs[d][144:272, 128:256]
        rows = packs[d][128:144, :].astype(F32)
        total = rows[0:1, :] + rows[1:2, :] + rows[2:3, :]
        ginv[at] = 1.0 / total


def qkv_kernel(normed, w, out):
    acc = jnp.zeros((256, 384), F32)
    for k in range(8):
        cols = [w[4 * k : 4 * k + 4, 64 * j : 64 * j + 64, :].reshape(256, 128) for j in range(3)]
        acc += jnp.dot(normed[k], jnp.concatenate(cols, axis=1), preferred_element_type=F32)
    q, k, v = acc[:, 0:128], acc[:, 128:256], acc[:, 256:384]
    low = left((256, 128))
    pairs = (jnp.where(low, q, half(k)), jnp.where(low, half(q), k))
    own, sib = v[0:128], v[128:256]
    low = left((128, 128))
    values = (jnp.where(low, own, half(sib)), jnp.where(low, half(own), sib))
    for g in range(2):
        qk = pairs[g].astype(BF)
        vv = values[g].astype(BF)
        for s in range(8):
            out[2 * s + g, 0:16, :] = qk[16 * s : 16 * s + 16, :]
            out[2 * s + g, 16:32, :] = qk[128 + 16 * s : 144 + 16 * s, :]
            out[2 * s + g, 32:48, :] = vv[16 * s : 16 * s + 16, :]


def attend_kernel(got, out):
    qk_own = got[:, 0:16, :].reshape(256, 128)
    qk_sib = got[:, 16:32, :].reshape(256, 128)
    vv = got[:, 32:48, :].reshape(256, 128)
    low = left((256, 128))

    def mix(qk):
        query = (jnp.where(low, 0.0, half(qk.astype(F32))) * (1.0 / HD**0.5)).astype(BF)
        first = lax.dot_general(query, qk_own, NT, preferred_element_type=F32)
        second = lax.dot_general(query, qk_sib, NT, preferred_element_type=F32)
        top = jnp.maximum(
            jnp.max(first, axis=1, keepdims=True), jnp.max(second, axis=1, keepdims=True)
        )
        first = jnp.exp(first - top)
        second = jnp.exp(second - top)
        total = jnp.sum(first, axis=1, keepdims=True) + jnp.sum(second, axis=1, keepdims=True)
        one = jnp.dot(first.astype(BF), vv, preferred_element_type=F32)
        two = jnp.dot(second.astype(BF), vv, preferred_element_type=F32)
        return (one + half(two)) / total

    mixed = jnp.where(low, mix(qk_own), half(mix(qk_sib)))
    out[...] = mixed.astype(BF).reshape(16, 16, 128)


def heads_of(got, own):
    a = got[:, 0].reshape(128, 128).astype(F32)
    b = got[:, 1].reshape(128, 128).astype(F32)
    low = left((128, 128))
    if own:
        return jnp.where(low, a, half(b)).astype(BF)
    return jnp.where(low, half(a), b).astype(BF)


def give_kernel(got, w, out):
    rows = heads_of(got, False)
    out[...] = lax.dot_general(
        rows, w[...].reshape(D, 128), NT, preferred_element_type=F32
    ).astype(BF)


def keep_kernel(got, w, other, normal, out):
    rows = heads_of(got, True)
    total = lax.dot_general(rows, w[...].reshape(D, 128), NT, preferred_element_type=F32)
    total = (total + other[...].astype(F32)).astype(BF)
    for z in range(8):
        out[z, 0:128, :] = total[:, 256 * z : 256 * z + 256]
    out[:, 128:176, :] = normal[...]


def normal_kernel(obs, out, hot, high, lows):
    low = left((16, 128))
    cells = lax.broadcasted_iota(jnp.int32, (128, 128), 0)
    for pair in range(16):
        a = obs[2 * pair].astype(F32)
        b = obs[2 * pair + 1].astype(F32)
        one = jnp.where(low, a, half(b))
        two = jnp.where(low, half(a), b)
        patch = one[0:1].astype(jnp.int32)
        base = two[0:1].astype(jnp.int32)
        w0 = one[1:2] + one[4:5]
        w1 = two[1:2] + two[4:5]
        w2 = one[2:3] + one[5:6]
        w3 = two[2:3] + two[5:6]
        v = one[3:4] + two[3:4]
        rel = cells - base
        e0, e1, e2, e3 = rel == 0, rel == 1, rel == 16, rel == 17
        zero = jnp.zeros((128, 128), F32)

        def place(x0, x1, x2, x3):
            out = zero
            for e, x in ((e0, x0), (e1, x1), (e2, x2), (e3, x3)):
                if x is not None:
                    out = jnp.where(e, x, out)
            return out

        terms = (
            place(w0 * w0, w1 * w1, w2 * w2, w3 * w3),
            place(w0 * w1, None, w2 * w3, None),
            place(None, w1 * w2, None, None),
            place(w0 * w2, w1 * w3, None, None),
            place(w0 * w3, None, None, None),
            place(v * w0, v * w1, v * w2, v * w3),
        )
        at = slice(128 * pair, 128 * pair + 128)
        hot[:, at] = jnp.where(cells == patch, 1.0, 0.0).astype(BF)
        for i, term in enumerate(terms):
            top = term.astype(BF)
            high[128 * i : 128 * i + 128, at] = top
            lows[128 * i : 128 * i + 128, at] = (term - top.astype(F32)).astype(BF)
    total = lax.dot_general(hot[...], high[...], NT, preferred_element_type=F32)
    total += lax.dot_general(hot[...], lows[...], NT, preferred_element_type=F32)
    total = total.astype(BF)
    for w in range(8):
        for i in range(6):
            out[w, 16 * (i % 3) : 16 * (i % 3) + 16, 128 * (i // 3) : 128 * (i // 3) + 128] = total[
                16 * w : 16 * w + 16, 128 * i : 128 * i + 128
            ]


def resid_kernel(got, x, gain, resid, out):
    attn = got[0, 0:128, :].astype(F32)
    normal = got[0, 128:176, :].astype(F32)
    for k in range(1, 8):
        attn += got[k, 0:128, :].astype(F32)
        normal += got[k, 128:176, :].astype(F32)
    total = x[...].astype(F32) + attn
    resid[...] = total
    scaled = (total * gain[...]).astype(BF)
    normal = normal.astype(BF)
    for k in range(8):
        out[k, 0:128, :] = scaled
        out[k, 128:176, :] = normal


def ffn_kernel(got, ginv, up, down, wdec, resid, own_dec, out, acc, scale):
    step = pl.program_id(0)

    @pl.when(step == 0)
    def _():
        squares = jnp.zeros((128, 1), F32)
        for k in range(8):
            a = got[k, 0:128, :].astype(F32) * ginv[k]
            squares += jnp.sum(a * a, axis=1, keepdims=True)
        scale[...] = jnp.broadcast_to(lax.rsqrt(squares / D + EPS), (128, 128))

    wide = jnp.concatenate([got[k, 0:128, :] for k in range(8)], axis=1)
    pre = jnp.dot(wide, up[...], preferred_element_type=F32) * scale[:, 0:1]
    hidden = 0.5 * pre * (1.0 + jnp.tanh(GELU * (pre + 0.044715 * (pre * pre * pre))))
    part = jnp.dot(hidden.astype(BF), down[...], preferred_element_type=F32)

    @pl.when(step == 0)
    def _():
        acc[...] = part

    @pl.when(step > 0)
    def _():
        acc[...] += part

    @pl.when(step == pl.num_programs(0) - 1)
    def _():
        total = acc[...].astype(BF)
        decoded = jnp.dot(total, wdec[...].reshape(D, 128), preferred_element_type=F32)
        decoded += jnp.dot(resid[...].astype(BF), own_dec[...], preferred_element_type=F32)
        decoded = decoded.astype(BF)
        for z in range(8):
            out[z, :, 0:256] = total[:, 256 * z : 256 * z + 256]
            out[z, :, 256:384] = decoded


def final_kernel(got, resid, normal, own_dec, state, guidance):
    total = resid[...]
    decoded = jnp.zeros((128, 128), F32)
    for k in range(8):
        total += got[k, :, 0:256].astype(F32)
        decoded += got[k, :, 256:384].astype(F32)
    state[...] = total.astype(BF)

    def diag(i):
        rows = slice(16 * (i % 3), 16 * (i % 3) + 16)
        cols = slice(128 * (i // 3), 128 * (i // 3) + 128)
        return normal[:, rows, cols].reshape(128, 128).astype(F32)

    grad = diag(0) * decoded - diag(5)
    for i, d in enumerate(STEPS):
        if i:
            a = diag(i)
            grad += a * pltpu.roll(decoded, 128 - d, 1) + pltpu.roll(a * decoded, d, 1)
    guidance[...] = lax.dot_general(
        grad,
        own_dec[...].astype(F32),
        NT,
        precision=lax.Precision.HIGHEST,
        preferred_element_type=F32,
    )


def sds(shape, dtype=BF):
    return jax.ShapeDtypeStruct(shape, dtype)


def body(
    states,
    w_qkv,
    w_out,
    w_up,
    w_down,
    w_dec,
    gain_attn,
    gain_mlp,
    obs_patch,
    obs_base,
    obs_count,
    obs_weight,
    obs_value,
):
    n_tok, n_mlp = 32, 8
    x = states.reshape(128, 256)
    me = lax.axis_index("mlp").astype(jnp.int32).reshape(1)
    pairs = [(i, i ^ 1) for i in range(n_tok)]
    chips = [[2 * i + c for i in range(16)] for c in range(2)]

    live = jnp.arange(64, dtype=jnp.int32)[None, :] < obs_count[0][:, None]
    weights = jnp.where(live[:, None, :], obs_weight[0], 0.0)
    values = jnp.where(live, obs_value[0], 0.0)
    weights_hi = lax.reduce_precision(weights, 8, 7)
    values_hi = lax.reduce_precision(values, 8, 7)
    rows = [
        jnp.concatenate([obs_patch[0], obs_base[0]], axis=1).astype(F32)[:, None, :],
        weights_hi.reshape(32, 2, 128),
        jnp.concatenate([values_hi, values - values_hi], axis=1)[:, None, :],
        (weights - weights_hi).reshape(32, 2, 128),
        jnp.zeros((32, 10, 128), F32),
    ]
    obs = jnp.concatenate(rows, axis=1).astype(BF)

    send = pl.pallas_call(pack_kernel, out_shape=sds((32, 272, 128)), compiler_params=params(24))(
        w_qkv, w_out.T, obs
    )
    weights_in = lax.all_to_all(send, "tok", 0, 0, tiled=True)

    g_hi = lax.reduce_precision(gain_mlp, 8, 7)
    g_mid = lax.reduce_precision(gain_mlp - g_hi, 8, 7)
    g_low = gain_mlp - g_hi - g_mid
    gains = jnp.concatenate([jnp.stack([g_hi, g_mid, g_low]), jnp.zeros((13, 256), F32)], axis=0)
    pack = jnp.concatenate(
        [x, gains.astype(BF), jnp.concatenate([w_dec[:128], w_dec[128:]], axis=1)], axis=0
    )
    packs = [pack] + [
        lax.ppermute(pack, "mlp", [(i, (i + d) % n_mlp) for i in range(n_mlp)])
        for d in range(1, n_mlp)
    ]
    sibling = lax.ppermute(jnp.stack([p[:128] for p in packs]), "tok", pairs)
    normed, wdec, ginv = pl.pallas_call(
        norm_kernel,
        out_shape=(sds((8, 256, 256)), sds((8, 256, 128)), sds((8, 1, 256), F32)),
        in_specs=[pl.BlockSpec(memory_space=pltpu.SMEM)]
        + [pl.BlockSpec(memory_space=pltpu.VMEM)] * 10,
        compiler_params=params(24),
    )(me, *packs, sibling, gain_attn.reshape(8, 1, 256))

    qkv = pl.pallas_call(
        qkv_kernel,
        grid=(1,),
        in_specs=[
            pl.BlockSpec((8, 256, 256), lambda i: (0, 0, 0)),
            pl.BlockSpec((32, 192, 128), lambda i: (0, 0, 0)),
        ],
        out_specs=pl.BlockSpec((16, 48, 128), lambda i: (0, 0, 0)),
        out_shape=sds((16, 48, 128)),
        compiler_params=params(24),
    )(normed, weights_in)
    qkv_in = lax.all_to_all(qkv, "tok", 0, 0, tiled=True, axis_index_groups=chips)

    normal = pl.pallas_call(
        normal_kernel,
        grid=(1,),
        in_specs=[pl.BlockSpec((32, 16, 128), lambda i: (0, 16, 0))],
        out_specs=pl.BlockSpec((8, 48, 256), lambda i: (0, 0, 0)),
        out_shape=sds((8, 48, 256)),
        scratch_shapes=[
            pltpu.VMEM((128, 2048), BF),
            pltpu.VMEM((768, 2048), BF),
            pltpu.VMEM((768, 2048), BF),
        ],
        compiler_params=params(24),
    )(weights_in)

    attended = pl.pallas_call(
        attend_kernel, out_shape=sds((16, 16, 128)), compiler_params=params(24)
    )(qkv_in)
    back = lax.all_to_all(attended, "tok", 0, 0, tiled=True, axis_index_groups=chips)
    back = back.reshape(8, 2, 16, 128)

    out_spec = pl.BlockSpec((32, 64, 128), lambda i: (0, 3, 0))
    back_spec = pl.BlockSpec((8, 2, 16, 128), lambda i: (0, 0, 0, 0))
    flat_spec = pl.BlockSpec((128, D), lambda i: (0, 0))
    give = pl.pallas_call(
        give_kernel,
        grid=(1,),
        in_specs=[back_spec, out_spec],
        out_specs=flat_spec,
        out_shape=sds((128, D)),
        compiler_params=params(24),
    )(back, weights_in)
    taken = lax.ppermute(give, "tok", pairs)
    shares = pl.pallas_call(
        keep_kernel,
        grid=(1,),
        in_specs=[
            back_spec,
            out_spec,
            flat_spec,
            pl.BlockSpec((8, 48, 256), lambda i: (0, 0, 0)),
        ],
        out_specs=pl.BlockSpec((8, 176, 256), lambda i: (0, 0, 0)),
        out_shape=sds((8, 176, 256)),
        compiler_params=params(24),
    )(back, weights_in, taken, normal)
    shares_in = lax.all_to_all(shares, "mlp", 0, 0, tiled=True)

    resid, scaled = pl.pallas_call(
        resid_kernel,
        out_shape=(sds((128, 256), F32), sds((8, 176, 256))),
        compiler_params=params(24),
    )(shares_in, x, gain_mlp.reshape(1, 256))
    wide = lax.all_to_all(scaled, "mlp", 0, 0, tiled=True)

    whole = lambda *shape: pl.BlockSpec(shape, lambda i: (0,) * len(shape))
    chunk = 256
    down = pl.pallas_call(
        ffn_kernel,
        grid=(1024 // chunk,),
        in_specs=[
            whole(8, 176, 256),
            whole(8, 1, 256),
            pl.BlockSpec((D, chunk), lambda i: (0, i)),
            pl.BlockSpec((chunk, D), lambda i: (i, 0)),
            whole(8, 256, 128),
            whole(128, 256),
            whole(256, 128),
        ],
        out_specs=whole(8, 128, 384),
        out_shape=sds((8, 128, 384)),
        scratch_shapes=[pltpu.VMEM((128, D), F32), pltpu.VMEM((128, 128), F32)],
        compiler_params=params(32),
    )(wide, ginv, w_up, w_down, wdec, resid, w_dec)
    down_in = lax.all_to_all(down, "mlp", 0, 0, tiled=True)

    state, guidance = pl.pallas_call(
        final_kernel,
        grid=(1,),
        in_specs=[
            whole(8, 128, 384),
            whole(128, 256),
            whole(8, 48, 256),
            whole(256, 128),
        ],
        out_specs=(whole(128, 256), whole(128, 256)),
        out_shape=(sds((128, 256)), sds((128, 256), F32)),
        compiler_params=params(24),
    )(down_in, resid, wide[:, 128:176, :], w_dec)
    return state.reshape(8, 16, 256), guidance.reshape(8, 16, 256)


def solution(mesh):
    placed = (
        P(None, "tok", "mlp"),
        P("tok", "mlp"),
        P("mlp", "tok"),
        P(None, "mlp"),
        P("mlp", None),
        P("mlp", None),
        P(),
        P("mlp"),
        P(("tok", "mlp"), None, None),
        P(("tok", "mlp"), None, None),
        P(("tok", "mlp"), None),
        P(("tok", "mlp"), None, None, None),
        P(("tok", "mlp"), None, None),
    )
    return jax.shard_map(
        body,
        mesh=mesh,
        in_specs=placed,
        out_specs=(P(None, "tok", "mlp"), P(None, "tok", "mlp")),
        check_vma=False,
    )
```

```python
import functools

import jax
import jax.numpy as jnp
from jax import lax
from jax.experimental import pallas as pl
from jax.experimental.pallas import tpu as pltpu
from jax.sharding import PartitionSpec as P

D = 2048
HD = 64
EPS = 1e-06
BF = jnp.bfloat16
F32 = jnp.float32
NT = (((1,), (1,)), ((), ()))
GELU = 0.7978845608028654
STEPS = (0, 1, 15, 16, 17)


def params(mib):
    return pltpu.CompilerParams(vmem_limit_bytes=mib * 1024 * 1024)


def lanes(shape):
    return lax.broadcasted_iota(jnp.int32, shape, len(shape) - 1)


def half(x):
    return pltpu.roll(x, 64, 1)


def left(shape):
    return lanes(shape) < 64


def pack_kernel(counts, wqkv, wout_t, x, gain, wdec, patch, base, weight, value, out, pack):
    n = out.shape[0]
    slots = lanes((4, 64))
    zero = jnp.zeros((1, 64), F32)
    rest = jnp.zeros((12, 128), F32)
    for dest in range(n):
        c = dest % 2
        for j in range(3):
            out[dest, 64 * j : 64 * j + 64, :] = wqkv[:, 256 * j + 128 * c : 256 * j + 128 * c + 128]
        out[dest, 192:256, :] = wout_t[:, 128 * c : 128 * c + 128]
        row = slice(dest, dest + 1)
        live = slots < counts[0, dest]
        w = jnp.where(live, weight[0, dest], 0.0)
        v = jnp.where(live[0:1], value[0, row, :], 0.0)
        other = [v, patch[0, row, :].astype(F32), base[0, row, :].astype(F32), zero]
        both = jnp.concatenate([w, jnp.concatenate(other, axis=0)], axis=1)
        out[dest, 256:272, :] = jnp.concatenate([both, rest], axis=0).astype(BF)
    pack[0:128, :] = x[...]
    g = gain[...]
    high = g.astype(BF).astype(F32)
    mid = (g - high).astype(BF).astype(F32)
    low = g - high - mid
    pack[128:144, :] = jnp.concatenate([high, mid, low, jnp.zeros((13, 256), F32)], axis=0).astype(BF)
    pack[144:272, 0:128] = wdec[0:128, :]
    pack[144:272, 128:256] = wdec[128:256, :]


def norm_kernel(me, *refs):
    packs, gain = refs[:8], refs[8]
    normed, wdec, ginv = refs[9:]
    m = me[0]
    squares = jnp.zeros((128, 1), F32)
    for d in range(8):
        a = packs[d][0:128, :].astype(F32)
        squares += jnp.sum(a * a, axis=1, keepdims=True)
    r = lax.rsqrt(squares / D + EPS)
    for d in range(8):
        at = lax.rem(m - d + 8, 8)
        normed[at] = (packs[d][0:128, :].astype(F32) * r * gain[at]).astype(BF)
        wdec[at, 0:128, :] = packs[d][144:272, 0:128]
        wdec[at, 128:256, :] = packs[d][144:272, 128:256]
        rows = packs[d][128:144, :].astype(F32)
        ginv[at] = 1.0 / (rows[0:1, :] + rows[1:2, :] + rows[2:3, :])


def qkv_kernel(mine, sibling, w, out, slots):
    acc = jnp.zeros((256, 384), F32)
    for k in range(8):
        cols = [w[4 * k : 4 * k + 4, 64 * j : 64 * j + 64, :].reshape(256, 128) for j in range(3)]
        rows = jnp.concatenate([mine[k], sibling[k]], axis=0)
        acc += jnp.dot(rows, jnp.concatenate(cols, axis=1), preferred_element_type=F32)
    q, k, v = acc[:, 0:128], acc[:, 128:256], acc[:, 256:384]
    low = left((256, 128))
    pairs = (jnp.where(low, q, half(k)), jnp.where(low, half(q), k))
    own, sib = v[0:128], v[128:256]
    low = left((128, 128))
    values = (jnp.where(low, own, half(sib)), jnp.where(low, half(own), sib))
    for g in range(2):
        qk = pairs[g].astype(BF)
        vv = values[g].astype(BF)
        for s in range(8):
            out[2 * s + g, 0:16, :] = qk[16 * s : 16 * s + 16, :]
            out[2 * s + g, 16:32, :] = qk[128 + 16 * s : 144 + 16 * s, :]
            out[2 * s + g, 32:48, :] = vv[16 * s : 16 * s + 16, :]
    low = left((16, 128))
    tiles = []
    for pair in range(16):
        a = w[2 * pair, 256:272, :].astype(F32)
        b = w[2 * pair + 1, 256:272, :].astype(F32)
        tiles.append(jnp.where(low, a, half(b))[0:4])
        tiles.append(jnp.where(low, half(a), b)[0:4])
    slots[...] = jnp.concatenate(tiles, axis=0).astype(BF)


def attend_kernel(got, out):
    qk_own = got[:, 0:16, :].reshape(256, 128)
    qk_sib = got[:, 16:32, :].reshape(256, 128)
    vv = got[:, 32:48, :].reshape(256, 128)
    low = left((256, 128))

    def mix(qk):
        query = (jnp.where(low, 0.0, half(qk.astype(F32))) * (1.0 / HD**0.5)).astype(BF)
        first = lax.dot_general(query, qk_own, NT, preferred_element_type=F32)
        second = lax.dot_general(query, qk_sib, NT, preferred_element_type=F32)
        top = jnp.maximum(
            jnp.max(first, axis=1, keepdims=True), jnp.max(second, axis=1, keepdims=True)
        )
        first = jnp.exp(first - top)
        second = jnp.exp(second - top)
        total = jnp.sum(first, axis=1, keepdims=True) + jnp.sum(second, axis=1, keepdims=True)
        one = jnp.dot(first.astype(BF), vv, preferred_element_type=F32)
        two = jnp.dot(second.astype(BF), vv, preferred_element_type=F32)
        return (one + half(two)) / total

    mixed = jnp.where(low, mix(qk_own), half(mix(qk_sib)))
    out[...] = mixed.astype(BF).reshape(16, 16, 128)


def heads_of(got, own):
    a = got[:, 0].reshape(128, 128).astype(F32)
    b = got[:, 1].reshape(128, 128).astype(F32)
    low = left((128, 128))
    if own:
        return jnp.where(low, a, half(b)).astype(BF)
    return jnp.where(low, half(a), b).astype(BF)


def give_kernel(got, w, out):
    rows = heads_of(got, False)
    out[...] = lax.dot_general(
        rows, w[...].reshape(D, 128), NT, preferred_element_type=F32
    ).astype(BF)


def keep_kernel(got, w, other, out):
    rows = heads_of(got, True)
    total = lax.dot_general(rows, w[...].reshape(D, 128), NT, preferred_element_type=F32)
    total = (total + other[...].astype(F32)).astype(BF)
    for z in range(8):
        out[z] = total[:, 256 * z : 256 * z + 256]


def normal_kernel(*refs):
    n = len(refs) - 4
    slots, start, out, hot, terms = refs[:n], refs[n], refs[n + 1], refs[n + 2], refs[n + 3]
    cells = lax.broadcasted_iota(jnp.int32, (128, 128), 0).astype(F32).astype(BF)
    zero = jnp.zeros((128, 128), BF)
    one = jnp.ones((128, 128), BF)

    def place(*picks):
        out = zero
        for e, x in picks:
            out = jnp.where(e, jnp.broadcast_to(x.astype(BF), (128, 128)), out)
        return out

    total = start[...]
    for k in range(n):

        def pair(i, _):
            rows = slots[k][pl.ds(pl.multiple_of(16 * i, 16), 16), :].astype(F32)
            for h in range(2):
                t = rows[8 * h : 8 * h + 8]
                w0, w1, w2, w3, v = (t[j : j + 1] for j in range(5))
                rel = cells - jnp.broadcast_to(t[6:7].astype(BF), (128, 128))
                e0, e1, e2, e3 = rel == 0, rel == 1, rel == 16, rel == 17
                parts = (
                    place((e0, w0 * w0), (e1, w1 * w1), (e2, w2 * w2), (e3, w3 * w3)),
                    place((e0, w0 * w1), (e2, w2 * w3)),
                    place((e1, w1 * w2)),
                    place((e0, w0 * w2), (e1, w1 * w3)),
                    place((e0, w0 * w3)),
                    place((e0, v * w0), (e1, v * w1), (e2, v * w2), (e3, v * w3)),
                )
                at = pl.ds(pl.multiple_of(256 * i + 128 * h, 128), 128)
                patch = jnp.broadcast_to(t[5:6].astype(BF), (128, 128))
                hot[:, at] = jnp.where(cells == patch, one, zero)
                for j, part in enumerate(parts):
                    terms[128 * j : 128 * j + 128, at] = part
            return 0

        lax.fori_loop(0, 8, pair, 0)
        total += lax.dot_general(hot[...], terms[...], NT, preferred_element_type=F32)
    out[...] = total


def resid_kernel(got, x, gain, resid, out):
    total = x[...].astype(F32)
    for k in range(8):
        total += got[k].astype(F32)
    resid[...] = total
    scaled = (total * gain[...]).astype(BF)
    for k in range(8):
        out[k] = scaled


def ffn_kernel(got, ginv, up, down, wdec, resid, own_dec, out):
    squares = jnp.zeros((128, 1), F32)
    for k in range(8):
        a = got[k].astype(F32) * ginv[k]
        squares += jnp.sum(a * a, axis=1, keepdims=True)
    scale = lax.rsqrt(squares / D + EPS)
    wide = jnp.concatenate([got[k] for k in range(8)], axis=1)
    hidden = []
    for i in range(4):
        pre = jnp.dot(wide, up[:, 256 * i : 256 * i + 256], preferred_element_type=F32) * scale
        act = 0.5 * pre * (1.0 + jnp.tanh(GELU * (pre + 0.044715 * (pre * pre * pre))))
        hidden.append(act.astype(BF))
    hidden = jnp.concatenate(hidden, axis=1)
    decoded = jnp.dot(resid[...].astype(BF), own_dec[...], preferred_element_type=F32)
    for z in range(8):
        part = jnp.dot(hidden, down[:, 256 * z : 256 * z + 256], preferred_element_type=F32)
        part = part.astype(BF)
        out[z, :, 0:256] = part
        decoded += jnp.dot(part, wdec[z], preferred_element_type=F32)
    decoded = decoded.astype(BF)
    for z in range(8):
        out[z, :, 256:384] = decoded


def final_kernel(got, resid, normal, own_dec, state, guidance):
    total = resid[...]
    decoded = jnp.zeros((128, 128), F32)
    for k in range(8):
        total += got[k, :, 0:256].astype(F32)
        decoded += got[k, :, 256:384].astype(F32)
    state[...] = total.astype(BF)
    grad = normal[:, 0:128] * decoded - normal[:, 640:768]
    for i, d in enumerate(STEPS):
        if i:
            a = normal[:, 128 * i : 128 * i + 128]
            grad += a * pltpu.roll(decoded, 128 - d, 1) + pltpu.roll(a * decoded, d, 1)
    guidance[...] = lax.dot_general(
        grad,
        own_dec[...].astype(F32),
        NT,
        precision=lax.Precision.HIGHEST,
        preferred_element_type=F32,
    )


def sds(shape, dtype=BF):
    return jax.ShapeDtypeStruct(shape, dtype)


def body(
    states,
    w_qkv,
    w_out,
    w_up,
    w_down,
    w_dec,
    gain_attn,
    gain_mlp,
    obs_patch,
    obs_base,
    obs_count,
    obs_weight,
    obs_value,
):
    n_tok, n_mlp = 32, 8
    x = states.reshape(128, 256)
    me = lax.axis_index("mlp").astype(jnp.int32).reshape(1)
    pairs = [(i, i ^ 1) for i in range(n_tok)]
    chips = [[2 * i + c for i in range(16)] for c in range(2)]
    ring = [[(i, (i + d) % n_mlp) for i in range(n_mlp)] for d in range(n_mlp)]
    vmem = pl.BlockSpec(memory_space=pltpu.VMEM)
    smem = pl.BlockSpec(memory_space=pltpu.SMEM)
    whole = lambda *shape: pl.BlockSpec(shape, lambda i: (0,) * len(shape))

    send, pack = pl.pallas_call(
        pack_kernel,
        in_specs=[smem] + [vmem] * 9,
        out_shape=(sds((32, 272, 128)), sds((272, 256))),
        compiler_params=params(8),
    )(
        obs_count,
        w_qkv,
        w_out.T,
        x,
        gain_mlp.reshape(1, 256),
        w_dec,
        obs_patch,
        obs_base,
        obs_weight,
        obs_value,
    )
    weights_in = lax.all_to_all(send, "tok", 0, 0, tiled=True)
    packs = [pack] + [lax.ppermute(pack, "mlp", ring[d]) for d in range(1, n_mlp)]
    normed, wdec, ginv = pl.pallas_call(
        norm_kernel,
        out_shape=(sds((8, 128, 256)), sds((8, 256, 128)), sds((8, 1, 256), F32)),
        in_specs=[smem] + [vmem] * 9,
        compiler_params=params(8),
    )(me, *packs, gain_attn.reshape(8, 1, 256))
    sibling = lax.ppermute(normed, "tok", pairs)

    qkv, slots = pl.pallas_call(
        qkv_kernel,
        out_shape=(sds((16, 48, 128)), sds((128, 128))),
        compiler_params=params(8),
    )(normed, sibling, weights_in)
    qkv_in = lax.all_to_all(qkv, "tok", 0, 0, tiled=True, axis_index_groups=chips)
    slots_in = [slots] + [lax.ppermute(slots, "mlp", ring[d]) for d in range(1, n_mlp)]

    attended = pl.pallas_call(
        attend_kernel, out_shape=sds((16, 16, 128)), compiler_params=params(8)
    )(qkv_in)
    back = lax.all_to_all(attended, "tok", 0, 0, tiled=True, axis_index_groups=chips)
    back = back.reshape(8, 2, 16, 128)

    out_spec = pl.BlockSpec((32, 64, 128), lambda i: (0, 3, 0))
    give = pl.pallas_call(
        give_kernel,
        grid=(1,),
        in_specs=[whole(8, 2, 16, 128), out_spec],
        out_specs=whole(128, D),
        out_shape=sds((128, D)),
        compiler_params=params(8),
    )(back, weights_in)
    taken = lax.ppermute(give, "tok", pairs)
    shares = pl.pallas_call(
        keep_kernel,
        grid=(1,),
        in_specs=[whole(8, 2, 16, 128), out_spec, whole(128, D)],
        out_specs=whole(8, 128, 256),
        out_shape=sds((8, 128, 256)),
        compiler_params=params(8),
    )(back, weights_in, taken)
    shares_in = lax.all_to_all(shares, "mlp", 0, 0, tiled=True)

    def normals(parts, start):
        return pl.pallas_call(
            normal_kernel,
            out_shape=sds((128, 768), F32),
            scratch_shapes=[pltpu.VMEM((128, 2048), BF), pltpu.VMEM((768, 2048), BF)],
            compiler_params=params(12),
            cost_estimate=pl.CostEstimate(
                flops=len(parts) * 500_000_000, bytes_accessed=1_000_000, transcendentals=0
            ),
        )(*parts, start)

    normal = normals(slots_in[:4], jnp.zeros((128, 768), F32))
    shares_in, normal = lax.optimization_barrier((shares_in, normal))

    resid, scaled = pl.pallas_call(
        resid_kernel,
        out_shape=(sds((128, 256), F32), sds((8, 128, 256))),
        compiler_params=params(8),
    )(shares_in, x, gain_mlp.reshape(1, 256))
    wide = lax.all_to_all(scaled, "mlp", 0, 0, tiled=True)
    normal = normals(slots_in[4:], normal)
    wide, normal = lax.optimization_barrier((wide, normal))

    down = pl.pallas_call(
        ffn_kernel, out_shape=sds((8, 128, 384)), compiler_params=params(24)
    )(wide, ginv, w_up, w_down, wdec, resid, w_dec)
    down_in = lax.all_to_all(down, "mlp", 0, 0, tiled=True)

    state, guidance = pl.pallas_call(
        final_kernel,
        out_shape=(sds((128, 256)), sds((128, 256), F32)),
        compiler_params=params(8),
    )(down_in, resid, normal, w_dec)
    return state.reshape(8, 16, 256), guidance.reshape(8, 16, 256)


def solution(mesh):
    placed = (
        P(None, "tok", "mlp"),
        P("tok", "mlp"),
        P("mlp", "tok"),
        P(None, "mlp"),
        P("mlp", None),
        P("mlp", None),
        P(),
        P("mlp"),
        P(("tok", "mlp"), None, None),
        P(("tok", "mlp"), None, None),
        P(("tok", "mlp"), None),
        P(("tok", "mlp"), None, None, None),
        P(("tok", "mlp"), None, None),
    )
    return jax.shard_map(
        body,
        mesh=mesh,
        in_specs=placed,
        out_specs=(P(None, "tok", "mlp"), P(None, "tok", "mlp")),
        check_vma=False,
    )
```

```python
import functools

import jax
import jax.numpy as jnp
from jax import lax
from jax.experimental import pallas as pl
from jax.experimental.pallas import tpu as pltpu
from jax.sharding import PartitionSpec as P

D = 2048
HD = 64
EPS = 1e-06
BF = jnp.bfloat16
F32 = jnp.float32
NT = (((1,), (1,)), ((), ()))
GELU = 0.7978845608028654
STEPS = (0, 1, 15, 16, 17)


def params(mib):
    return pltpu.CompilerParams(vmem_limit_bytes=mib * 1024 * 1024)


def lanes(shape):
    return lax.broadcasted_iota(jnp.int32, shape, len(shape) - 1)


def half(x):
    return pltpu.roll(x, 64, 1)


def left(shape):
    return lanes(shape) < 64


def fetch(pairs, sem):
    copies = [pltpu.make_async_copy(src, dst, sem.at[i]) for i, (src, dst) in enumerate(pairs)]
    for copy in copies:
        copy.start()
    for copy in copies:
        copy.wait()


def pack_kernel(*refs):
    ins, out, bufs, counts, sem = refs[:7], refs[7], refs[8:16], refs[16], refs[17]
    wqkv, wout_t, patch, base, weight, value, blocks, obs = bufs
    dests = [*bufs[:6], counts]
    loads = [pltpu.make_async_copy(ins[i], dests[i], sem.at[i]) for i in range(7)]
    for load in loads:
        load.start()
    loads[0].wait()
    loads[1].wait()
    for c in range(2):
        for j in range(3):
            blocks[c, 64 * j : 64 * j + 64, :] = wqkv[:, 256 * j + 128 * c : 256 * j + 128 * c + 128]
        blocks[c, 192:256, :] = wout_t[:, 128 * c : 128 * c + 128]
    n = out.shape[0]
    copies = [
        pltpu.make_async_copy(blocks.at[d % 2], out.at[d, pl.ds(0, 256), :], sem.at[7 + d])
        for d in range(n)
    ]
    for copy in copies:
        copy.start()
    for load in loads[2:]:
        load.wait()
    slots = lanes((4, 64))
    zero = jnp.zeros((1, 64), F32)
    rest = jnp.zeros((12, 128), F32)
    for dest in range(n):
        row = slice(dest, dest + 1)
        live = slots < counts[0, dest]
        w = jnp.where(live, weight[0, dest], 0.0)
        v = jnp.where(live[0:1], value[0, row, :], 0.0)
        other = [v, patch[0, row, :].astype(F32), base[0, row, :].astype(F32), zero]
        both = jnp.concatenate([w, jnp.concatenate(other, axis=0)], axis=1)
        obs[dest] = jnp.concatenate([both, rest], axis=0).astype(BF)
    last = pltpu.make_async_copy(obs, out.at[:, pl.ds(256, 16), :], sem.at[7 + n])
    last.start()
    for copy in copies:
        copy.wait()
    last.wait()


def shared_kernel(wdec, gain, out, w_buf, g_buf, buf, sem):
    fetch([(gain, g_buf), (wdec, w_buf)], sem)
    g = g_buf[...]
    high = g.astype(BF).astype(F32)
    mid = (g - high).astype(BF).astype(F32)
    rows = jnp.concatenate([high, mid, g - high - mid, jnp.zeros((13, 256), F32)], axis=0)
    buf[0:128, 0:128] = w_buf[0:128, :]
    buf[0:128, 128:256] = w_buf[128:256, :]
    buf[128:144, :] = rows.astype(BF)
    fetch([(buf, out)], sem)


def groups_of(me, core):
    turn = 1 - 2 * core[0]
    mine = [lax.rem(me[0] - turn * k + 8, 8) for k in (1, 2, 3)]
    theirs = [lax.rem(me[0] + turn * k + 8, 8) for k in (1, 2, 3)]
    return mine, theirs, lax.rem(me[0] + 4, 8)


def norm_kernel(me, core, *refs):
    x, other, far, far_sib, mine, theirs = *refs[:4], refs[4:7], refs[7:10]
    gain, out, buf, sem = refs[10:]
    near, across, opposite = groups_of(me, core)
    low, top = pl.ds(0, 128), pl.ds(128, 128)
    pairs = [
        (x, buf.at[me[0], low, :]),
        (other, buf.at[me[0], top, :]),
        (far, buf.at[opposite, low, :]),
        (far_sib, buf.at[opposite, top, :]),
    ]
    for k in range(3):
        pairs.append((mine[k], buf.at[near[k]]))
        pairs.append((theirs[k].at[top, :], buf.at[across[k], low, :]))
        pairs.append((theirs[k].at[low, :], buf.at[across[k], top, :]))
    fetch(pairs, sem)
    squares = jnp.zeros((256, 1), F32)
    for k in range(8):
        a = buf[k].astype(F32)
        squares += jnp.sum(a * a, axis=1, keepdims=True)
    r = lax.rsqrt(squares / D + EPS)
    for k in range(8):
        out[k] = (buf[k].astype(F32) * r * gain[k]).astype(BF)


def qkv_kernel(normed, w, out, slots):
    acc = jnp.zeros((256, 384), F32)
    for k in range(8):
        cols = [w[4 * k : 4 * k + 4, 64 * j : 64 * j + 64, :].reshape(256, 128) for j in range(3)]
        acc += jnp.dot(normed[k], jnp.concatenate(cols, axis=1), preferred_element_type=F32)
    q, k, v = acc[:, 0:128], acc[:, 128:256], acc[:, 256:384]
    low = left((256, 128))
    pairs = (jnp.where(low, q, half(k)), jnp.where(low, half(q), k))
    own, sib = v[0:128], v[128:256]
    low = left((128, 128))
    values = (jnp.where(low, own, half(sib)), jnp.where(low, half(own), sib))
    for g in range(2):
        qk = pairs[g].astype(BF)
        vv = values[g].astype(BF)
        for s in range(8):
            out[2 * s + g, 0:16, :] = qk[16 * s : 16 * s + 16, :]
            out[2 * s + g, 16:32, :] = qk[128 + 16 * s : 144 + 16 * s, :]
            out[2 * s + g, 32:48, :] = vv[16 * s : 16 * s + 16, :]
    low = left((16, 128))
    tiles = []
    for pair in range(16):
        a = w[2 * pair, 256:272, :].astype(F32)
        b = w[2 * pair + 1, 256:272, :].astype(F32)
        tiles.append(jnp.where(low, a, half(b))[0:4])
        tiles.append(jnp.where(low, half(a), b)[0:4])
    slots[:, 0:128] = jnp.concatenate(tiles[:16], axis=0).astype(BF)
    slots[:, 128:256] = jnp.concatenate(tiles[16:], axis=0).astype(BF)


def attend_kernel(got, out):
    qk_own = got[:, 0:16, :].reshape(256, 128)
    qk_sib = got[:, 16:32, :].reshape(256, 128)
    vv = got[:, 32:48, :].reshape(256, 128)
    low = left((256, 128))

    def mix(qk):
        query = (jnp.where(low, 0.0, half(qk.astype(F32))) * (1.0 / HD**0.5)).astype(BF)
        first = lax.dot_general(query, qk_own, NT, preferred_element_type=F32)
        second = lax.dot_general(query, qk_sib, NT, preferred_element_type=F32)
        top = jnp.maximum(
            jnp.max(first, axis=1, keepdims=True), jnp.max(second, axis=1, keepdims=True)
        )
        first = jnp.exp(first - top)
        second = jnp.exp(second - top)
        total = jnp.sum(first, axis=1, keepdims=True) + jnp.sum(second, axis=1, keepdims=True)
        one = jnp.dot(first.astype(BF), vv, preferred_element_type=F32)
        two = jnp.dot(second.astype(BF), vv, preferred_element_type=F32)
        return (one + half(two)) / total

    mixed = jnp.where(low, mix(qk_own), half(mix(qk_sib)))
    out[...] = mixed.astype(BF).reshape(16, 16, 128)


def heads_of(got, own):
    a = got[:, 0].reshape(128, 128).astype(F32)
    b = got[:, 1].reshape(128, 128).astype(F32)
    low = left((128, 128))
    if own:
        return jnp.where(low, a, half(b)).astype(BF)
    return jnp.where(low, half(a), b).astype(BF)


def give_kernel(got, w, out):
    rows = heads_of(got, False)
    out[...] = lax.dot_general(
        rows, w[...].reshape(D, 128), NT, preferred_element_type=F32
    ).astype(BF)


def keep_kernel(me, got, w, other, slots, *refs):
    outs, buf = refs[:8], refs[8]
    rows = heads_of(got, True)
    total = lax.dot_general(rows, w[...].reshape(D, 128), NT, preferred_element_type=F32)
    total = (total + other[...].astype(F32)).astype(BF)
    for z in range(8):
        buf[z] = total[:, 256 * z : 256 * z + 256]
    for d in range(8):
        outs[d][0:128, :] = buf[lax.rem(me[0] + d, 8)]
        outs[d][128:192, :] = slots[...]


def normal_kernel(slots, out, hot_a, hot_b, terms_a, terms_b):
    cells = lax.broadcasted_iota(jnp.int32, (128, 128), 0).astype(F32).astype(BF)
    zero = jnp.zeros((128, 128), BF)
    one = jnp.ones((128, 128), BF)

    def place(*picks):
        out = zero
        for e, x in picks:
            out = jnp.where(e, jnp.broadcast_to(x.astype(BF), (128, 128)), out)
        return out

    def build(step, hot, terms):
        group, first = lax.div(step, 4), lax.rem(step, 2) * 32
        side = pl.ds(pl.multiple_of(lax.div(lax.rem(step, 4), 2) * 128, 128), 128)
        for c in range(2):
            rows = slots[group, pl.ds(pl.multiple_of(first + 16 * c, 16), 16), side].astype(F32)
            for h in range(2):
                t = rows[8 * h : 8 * h + 8]
                w0, w1, w2, w3, v = (t[j : j + 1] for j in range(5))
                rel = cells - jnp.broadcast_to(t[6:7].astype(BF), (128, 128))
                e0, e1, e2, e3 = rel == 0, rel == 1, rel == 16, rel == 17
                parts = (
                    place((e0, w0 * w0), (e1, w1 * w1), (e2, w2 * w2), (e3, w3 * w3)),
                    place((e0, w0 * w1), (e2, w2 * w3)),
                    place((e1, w1 * w2)),
                    place((e0, w0 * w2), (e1, w1 * w3)),
                    place((e0, w0 * w3)),
                    place((e0, v * w0), (e1, v * w1), (e2, v * w2), (e3, v * w3)),
                )
                at = slice(256 * c + 128 * h, 256 * c + 128 * h + 128)
                patch = jnp.broadcast_to(t[5:6].astype(BF), (128, 128))
                hot[:, at] = jnp.where(cells == patch, one, zero)
                for j, part in enumerate(parts):
                    terms[128 * j : 128 * j + 128, at] = part

    def add(hot, terms):
        out[...] += lax.dot_general(hot[...], terms[...], NT, preferred_element_type=F32)

    out[...] = jnp.zeros(out.shape, F32)
    build(jnp.int32(0), hot_a, terms_a)

    def two(i, _):
        add(hot_a, terms_a)
        build(2 * i + 1, hot_b, terms_b)
        add(hot_b, terms_b)
        build(2 * i + 2, hot_a, terms_a)
        return 0

    lax.fori_loop(0, 15, two, 0)
    add(hot_a, terms_a)
    build(jnp.int32(31), hot_b, terms_b)
    add(hot_b, terms_b)


def resid_kernel(x, gain, *refs):
    got, (resid, scaled, slots) = refs[:8], refs[8:]
    total = x[...].astype(F32)
    for d in range(8):
        total += got[d][0:128, :].astype(F32)
        slots[d] = got[d][128:192, :]
    resid[...] = total
    out = (total * gain[...]).astype(BF)
    for k in range(8):
        scaled[k] = out


def ffn_kernel(me, core, got, *refs):
    own, far, mine, theirs = refs[0], refs[1], refs[2:5], refs[5:8]
    up, down, resid, own_dec, out, shared, sem = refs[8:]
    near, across, opposite = groups_of(me, core)
    pairs = [(own, shared.at[me[0]]), (far, shared.at[opposite])]
    for k in range(3):
        pairs.append((mine[k], shared.at[near[k]]))
        pairs.append((theirs[k], shared.at[across[k]]))
    fetch(pairs, sem)
    squares = jnp.zeros((128, 1), F32)
    for k in range(8):
        g = shared[k, 128:144, :].astype(F32)
        a = got[k].astype(F32) / (g[0:1] + g[1:2] + g[2:3])
        squares += jnp.sum(a * a, axis=1, keepdims=True)
    scale = lax.rsqrt(squares / D + EPS)
    wide = jnp.concatenate([got[k] for k in range(8)], axis=1)
    hidden = []
    for i in range(4):
        pre = jnp.dot(wide, up[:, 256 * i : 256 * i + 256], preferred_element_type=F32) * scale
        act = 0.5 * pre * (1.0 + jnp.tanh(GELU * (pre + 0.044715 * (pre * pre * pre))))
        hidden.append(act.astype(BF))
    hidden = jnp.concatenate(hidden, axis=1)
    decoded = jnp.dot(resid[...].astype(BF), own_dec[...], preferred_element_type=F32)
    for z in range(8):
        at = slice(256 * z, 256 * z + 256)
        part = jnp.dot(hidden, down[:, at], preferred_element_type=F32).astype(BF)
        out[z, :, 0:256] = part
        for i in range(2):
            side = slice(128 * i, 128 * i + 128)
            decoded += jnp.dot(part[:, side], shared[z, 0:128, side], preferred_element_type=F32)
    decoded = decoded.astype(BF)
    for z in range(8):
        out[z, :, 256:384] = decoded


def final_kernel(got, resid, normal, own_dec, state, guidance):
    total = resid[...]
    decoded = jnp.zeros((128, 128), F32)
    for k in range(8):
        total += got[k, :, 0:256].astype(F32)
        decoded += got[k, :, 256:384].astype(F32)
    state[...] = total.astype(BF)
    grad = normal[:, 0:128] * decoded - normal[:, 640:768]
    for i, d in enumerate(STEPS):
        if i:
            a = normal[:, 128 * i : 128 * i + 128]
            grad += a * pltpu.roll(decoded, 128 - d, 1) + pltpu.roll(a * decoded, d, 1)
    guidance[...] = lax.dot_general(
        grad,
        own_dec[...].astype(F32),
        NT,
        precision=lax.Precision.HIGHEST,
        preferred_element_type=F32,
    )


def stay(x):
    return pltpu.with_memory_space_constraint(x, pltpu.HBM)


def sds(shape, dtype=BF):
    return jax.ShapeDtypeStruct(shape, dtype)


def body(
    states,
    w_qkv,
    w_out,
    w_up,
    w_down,
    w_dec,
    gain_attn,
    gain_mlp,
    obs_patch,
    obs_base,
    obs_count,
    obs_weight,
    obs_value,
):
    n_tok, n_mlp = 32, 8
    x = states.reshape(128, 256)
    me = lax.axis_index("mlp").astype(jnp.int32).reshape(1)
    core = lax.rem(lax.axis_index("tok"), 2).astype(jnp.int32).reshape(1)
    pairs = [(i, i ^ 1) for i in range(n_tok)]
    chips = [[2 * i + c for i in range(16)] for c in range(2)]
    order = (1, 7, 2, 6, 3, 5, 4)
    ring = [[(i, (i + d) % n_mlp) for i in range(n_mlp)] for d in range(n_mlp)]
    vmem = pl.BlockSpec(memory_space=pltpu.VMEM)
    hbm = pl.BlockSpec(memory_space=pltpu.HBM)
    smem = pl.BlockSpec(memory_space=pltpu.SMEM)
    whole = lambda *shape: pl.BlockSpec(shape, lambda i: (0,) * len(shape))

    send = pl.pallas_call(
        pack_kernel,
        in_specs=[hbm] * 7,
        out_specs=hbm,
        out_shape=pltpu.HBM((32, 272, 128), BF),
        scratch_shapes=[
            pltpu.VMEM((64, 768), BF),
            pltpu.VMEM((64, 256), BF),
            pltpu.VMEM((1, 32, 64), jnp.int32),
            pltpu.VMEM((1, 32, 64), jnp.int32),
            pltpu.VMEM((1, 32, 4, 64), F32),
            pltpu.VMEM((1, 32, 64), F32),
            pltpu.VMEM((2, 256, 128), BF),
            pltpu.VMEM((32, 16, 128), BF),
            pltpu.SMEM((1, 32), jnp.int32),
            pltpu.SemaphoreType.DMA((40,)),
        ],
        compiler_params=params(8),
    )(*map(stay, (w_qkv, w_out.T, obs_patch, obs_base, obs_weight, obs_value, obs_count)))

    weights_in = lax.all_to_all(send, "tok", 0, 0, tiled=True)

    def shifted(k):
        return [
            (t * n_mlp + z, t * n_mlp + (z + (k if t % 2 == 0 else -k)) % n_mlp)
            for t in range(n_tok)
            for z in range(n_mlp)
        ]

    def gathered(near, far):
        mine = [lax.ppermute(near, ("tok", "mlp"), shifted(k)) for k in (1, 2, 3)]
        far_in = lax.ppermute(far, "mlp", ring[4])
        theirs = [lax.ppermute(r, "tok", pairs) for r in mine]
        return far_in, mine, theirs

    other = lax.ppermute(x, "tok", pairs)
    both, first, _ = lax.optimization_barrier((jnp.concatenate([x, other], axis=0), x, send))
    far_in, mine, theirs = gathered(both, first)
    normed = pl.pallas_call(
        norm_kernel,
        in_specs=[smem] * 2 + [hbm] * 10 + [vmem],
        out_shape=sds((8, 256, 256)),
        scratch_shapes=[pltpu.VMEM((8, 256, 256), BF), pltpu.SemaphoreType.DMA((13,))],
        compiler_params=params(8),
    )(
        me,
        core,
        *map(stay, (x, other, far_in, lax.ppermute(far_in, "tok", pairs), *mine, *theirs)),
        gain_attn.reshape(8, 1, 256),
    )
    shared = pl.pallas_call(
        shared_kernel,
        in_specs=[hbm] * 2,
        out_specs=hbm,
        out_shape=pltpu.HBM((144, 256), BF),
        scratch_shapes=[
            pltpu.VMEM((256, 128), BF),
            pltpu.VMEM((1, 256), F32),
            pltpu.VMEM((144, 256), BF),
            pltpu.SemaphoreType.DMA((2,)),
        ],
        compiler_params=params(4),
    )(stay(w_dec), stay(gain_mlp.reshape(1, 256)))
    shared, _ = lax.optimization_barrier((shared, both))
    far_shared, mine_shared, theirs_shared = gathered(shared, shared)
    weights_in, *others = lax.optimization_barrier(
        (weights_in, far_shared, *mine_shared, *theirs_shared)
    )

    qkv, slots = pl.pallas_call(
        qkv_kernel,
        out_shape=(sds((16, 48, 128)), sds((64, 256))),
        compiler_params=params(8),
    )(normed, weights_in)
    qkv_in = lax.all_to_all(qkv, "tok", 0, 0, tiled=True, axis_index_groups=chips)
    attended = pl.pallas_call(
        attend_kernel, out_shape=sds((16, 16, 128)), compiler_params=params(8)
    )(qkv_in)
    back = lax.all_to_all(attended, "tok", 0, 0, tiled=True, axis_index_groups=chips)
    back = back.reshape(8, 2, 16, 128)

    out_spec = pl.BlockSpec((32, 64, 128), lambda i: (0, 3, 0))
    give = pl.pallas_call(
        give_kernel,
        grid=(1,),
        in_specs=[whole(8, 2, 16, 128), out_spec],
        out_specs=whole(128, D),
        out_shape=sds((128, D)),
        compiler_params=params(8),
    )(back, weights_in)
    taken = lax.ppermute(give, "tok", pairs)
    shares = pl.pallas_call(
        keep_kernel,
        grid=(1,),
        in_specs=[smem, whole(8, 2, 16, 128), out_spec, whole(128, D), whole(64, 256)],
        out_specs=[whole(192, 256)] * 8,
        out_shape=[sds((192, 256))] * 8,
        scratch_shapes=[pltpu.VMEM((8, 128, 256), BF)],
        compiler_params=params(8),
    )(me, back, weights_in, taken, slots)
    shares_in = [shares[0]] + [lax.ppermute(shares[d], "mlp", ring[d]) for d in order]

    resid, scaled, slots_in = pl.pallas_call(
        resid_kernel,
        out_shape=(sds((128, 256), F32), sds((8, 128, 256)), sds((8, 64, 256))),
        compiler_params=params(8),
    )(x, gain_mlp.reshape(1, 256), *shares_in)
    wide = lax.all_to_all(scaled, "mlp", 0, 0, tiled=True)

    down_out = pl.pallas_call(
        ffn_kernel,
        in_specs=[smem] * 2 + [vmem] + [hbm] * 8 + [vmem] * 4,
        out_shape=sds((8, 128, 384)),
        scratch_shapes=[
            pltpu.VMEM((8, 144, 256), BF),
            pltpu.SemaphoreType.DMA((8,)),
        ],
        compiler_params=params(8),
    )(
        me,
        core,
        wide,
        *map(stay, (shared, *others)),
        w_up,
        w_down,
        resid,
        w_dec,
    )
    down_in = lax.all_to_all(down_out, "mlp", 0, 0, tiled=True)

    slots, _ = lax.optimization_barrier((slots_in, down_out))
    normal = pl.pallas_call(
        normal_kernel,
        grid=(1,),
        in_specs=[whole(8, 64, 256)],
        out_specs=whole(128, 768),
        out_shape=sds((128, 768), F32),
        scratch_shapes=[pltpu.VMEM((128, 512), BF)] * 2 + [pltpu.VMEM((768, 512), BF)] * 2,
        compiler_params=params(8),
        cost_estimate=pl.CostEstimate(
            flops=4_000_000_000, bytes_accessed=1_000_000, transcendentals=0
        ),
    )(slots)
    down_in, normal = lax.optimization_barrier((down_in, normal))

    state, guidance = pl.pallas_call(
        final_kernel,
        out_shape=(sds((128, 256)), sds((128, 256), F32)),
        compiler_params=params(8),
    )(down_in, resid, normal, w_dec)
    return state.reshape(8, 16, 256), guidance.reshape(8, 16, 256)


def solution(mesh):
    placed = (
        P(None, "tok", "mlp"),
        P("tok", "mlp"),
        P("mlp", "tok"),
        P(None, "mlp"),
        P("mlp", None),
        P("mlp", None),
        P(),
        P("mlp"),
        P(("tok", "mlp"), None, None),
        P(("tok", "mlp"), None, None),
        P(("tok", "mlp"), None),
        P(("tok", "mlp"), None, None, None),
        P(("tok", "mlp"), None, None),
    )
    return jax.shard_map(
        body,
        mesh=mesh,
        in_specs=placed,
        out_specs=(P(None, "tok", "mlp"), P(None, "tok", "mlp")),
        check_vma=False,
    )
```

```python
import functools

import jax
import jax.numpy as jnp
from jax import lax
from jax.experimental import pallas as pl
from jax.experimental.pallas import tpu as pltpu
from jax.sharding import PartitionSpec as P

D = 2048
HD = 64
EPS = 1e-06
BF = jnp.bfloat16
F32 = jnp.float32
NT = (((1,), (1,)), ((), ()))
GELU = 0.7978845608028654
STEPS = (0, 1, 15, 16, 17)


def params(mib):
    return pltpu.CompilerParams(vmem_limit_bytes=mib * 1024 * 1024)


def lanes(shape):
    return lax.broadcasted_iota(jnp.int32, shape, len(shape) - 1)


def half(x):
    return pltpu.roll(x, 64, 1)


def left(shape):
    return lanes(shape) < 64


def fetch(pairs, sem):
    copies = [pltpu.make_async_copy(src, dst, sem.at[i]) for i, (src, dst) in enumerate(pairs)]
    for copy in copies:
        copy.start()
    for copy in copies:
        copy.wait()


def pack_kernel(*refs):
    ins, out, bufs, counts, sem = refs[:7], refs[7], refs[8:16], refs[16], refs[17]
    wqkv, wout_t, patch, base, weight, value, blocks, obs = bufs
    dests = [*bufs[:6], counts]
    loads = [pltpu.make_async_copy(ins[i], dests[i], sem.at[i]) for i in range(7)]
    for load in loads:
        load.start()
    loads[0].wait()
    loads[1].wait()
    for c in range(2):
        for j in range(3):
            blocks[c, 64 * j : 64 * j + 64, :] = wqkv[:, 256 * j + 128 * c : 256 * j + 128 * c + 128]
        blocks[c, 192:256, :] = wout_t[:, 128 * c : 128 * c + 128]
    n = out.shape[0]
    copies = [
        pltpu.make_async_copy(blocks.at[d % 2], out.at[d, pl.ds(0, 256), :], sem.at[7 + d])
        for d in range(n)
    ]
    for copy in copies:
        copy.start()
    for load in loads[2:]:
        load.wait()
    slots = lanes((4, 64))
    zero = jnp.zeros((1, 64), F32)
    rest = jnp.zeros((12, 128), F32)
    for dest in range(n):
        row = slice(dest, dest + 1)
        live = slots < counts[0, dest]
        w = jnp.where(live, weight[0, dest], 0.0)
        v = jnp.where(live[0:1], value[0, row, :], 0.0)
        other = [v, patch[0, row, :].astype(F32), base[0, row, :].astype(F32), zero]
        both = jnp.concatenate([w, jnp.concatenate(other, axis=0)], axis=1)
        obs[dest] = jnp.concatenate([both, rest], axis=0).astype(BF)
    last = pltpu.make_async_copy(obs, out.at[:, pl.ds(256, 16), :], sem.at[7 + n])
    last.start()
    for copy in copies:
        copy.wait()
    last.wait()


def shared_kernel(wdec, gain, out, w_buf, g_buf, buf, sem):
    fetch([(gain, g_buf), (wdec, w_buf)], sem)
    g = g_buf[...]
    high = g.astype(BF).astype(F32)
    mid = (g - high).astype(BF).astype(F32)
    rows = jnp.concatenate([high, mid, g - high - mid, jnp.zeros((13, 256), F32)], axis=0)
    buf[0:128, 0:128] = w_buf[0:128, :]
    buf[0:128, 128:256] = w_buf[128:256, :]
    buf[128:144, :] = rows.astype(BF)
    fetch([(buf, out)], sem)


def groups_of(me, core):
    turn = 1 - 2 * core[0]
    mine = [lax.rem(me[0] - turn * k + 8, 8) for k in (1, 2, 3)]
    theirs = [lax.rem(me[0] + turn * k + 8, 8) for k in (1, 2, 3)]
    return mine, theirs, lax.rem(me[0] + 4, 8)


def norm_kernel(me, core, *refs):
    x, other, far, far_sib, mine, theirs = *refs[:4], refs[4:7], refs[7:10]
    gain, out, buf, sem = refs[10:]
    near, across, opposite = groups_of(me, core)
    low, top = pl.ds(0, 128), pl.ds(128, 128)
    pairs = [
        (x, buf.at[me[0], low, :]),
        (other, buf.at[me[0], top, :]),
        (far, buf.at[opposite, low, :]),
        (far_sib, buf.at[opposite, top, :]),
    ]
    for k in range(3):
        pairs.append((mine[k], buf.at[near[k]]))
        pairs.append((theirs[k].at[top, :], buf.at[across[k], low, :]))
        pairs.append((theirs[k].at[low, :], buf.at[across[k], top, :]))
    fetch(pairs, sem)
    squares = jnp.zeros((256, 1), F32)
    for k in range(8):
        a = buf[k].astype(F32)
        squares += jnp.sum(a * a, axis=1, keepdims=True)
    r = lax.rsqrt(squares / D + EPS)
    for k in range(8):
        out[k] = (buf[k].astype(F32) * r * gain[k]).astype(BF)


def qkv_kernel(normed, w, out, slots):
    acc = jnp.zeros((256, 384), F32)
    for k in range(8):
        cols = [w[4 * k : 4 * k + 4, 64 * j : 64 * j + 64, :].reshape(256, 128) for j in range(3)]
        acc += jnp.dot(normed[k], jnp.concatenate(cols, axis=1), preferred_element_type=F32)
    q, k, v = acc[:, 0:128], acc[:, 128:256], acc[:, 256:384]
    low = left((256, 128))
    pairs = (jnp.where(low, q, half(k)), jnp.where(low, half(q), k))
    own, sib = v[0:128], v[128:256]
    low = left((128, 128))
    values = (jnp.where(low, own, half(sib)), jnp.where(low, half(own), sib))
    for g in range(2):
        qk = pairs[g].astype(BF)
        vv = values[g].astype(BF)
        for s in range(8):
            out[2 * s + g, 0:16, :] = qk[16 * s : 16 * s + 16, :]
            out[2 * s + g, 16:32, :] = qk[128 + 16 * s : 144 + 16 * s, :]
            out[2 * s + g, 32:48, :] = vv[16 * s : 16 * s + 16, :]
    low = left((16, 128))
    tiles = []
    for pair in range(16):
        a = w[2 * pair, 256:272, :].astype(F32)
        b = w[2 * pair + 1, 256:272, :].astype(F32)
        tiles.append(jnp.where(low, a, half(b))[0:4])
        tiles.append(jnp.where(low, half(a), b)[0:4])
    slots[:, 0:128] = jnp.concatenate(tiles[:16], axis=0).astype(BF)
    slots[:, 128:256] = jnp.concatenate(tiles[16:], axis=0).astype(BF)


def attend_kernel(core, got, out):
    qk_own = got[:, 0:16, :].reshape(256, 128)
    qk_sib = got[:, 16:32, :].reshape(256, 128)
    vv = got[:, 32:48, :].reshape(256, 128)
    low = left((256, 128))

    def mix(qk):
        query = (jnp.where(low, 0.0, half(qk.astype(F32))) * (1.0 / HD**0.5)).astype(BF)
        first = lax.dot_general(query, qk_own, NT, preferred_element_type=F32)
        second = lax.dot_general(query, qk_sib, NT, preferred_element_type=F32)
        top = jnp.maximum(
            jnp.max(first, axis=1, keepdims=True), jnp.max(second, axis=1, keepdims=True)
        )
        first = jnp.exp(first - top)
        second = jnp.exp(second - top)
        total = jnp.sum(first, axis=1, keepdims=True) + jnp.sum(second, axis=1, keepdims=True)
        one = jnp.dot(first.astype(BF), vv, preferred_element_type=F32)
        two = jnp.dot(second.astype(BF), vv, preferred_element_type=F32)
        return (one + half(two)) / total

    c = core[0]
    out[:, c] = mix(qk_own).astype(BF).reshape(16, 16, 128)
    out[:, 1 - c] = mix(qk_sib).astype(BF).reshape(16, 16, 128)


def share_kernel(me, core, got, w, w_sib, slots, *refs):
    outs, buf = refs[:8], refs[8]
    low = left((128, 128))

    def heads_of(c):
        a = got[:, 0, c].reshape(128, 128).astype(F32)
        b = got[:, 1, c].reshape(128, 128).astype(F32)
        return jnp.where(low, a, half(b)).astype(BF)

    own, other = heads_of(core[0]), heads_of(1 - core[0])
    for z in range(8):
        at = slice(4 * z, 4 * z + 4)
        part = lax.dot_general(own, w[at].reshape(256, 128), NT, preferred_element_type=F32)
        part += lax.dot_general(other, w_sib[at].reshape(256, 128), NT, preferred_element_type=F32)
        buf[z] = part.astype(BF)
    for d in range(8):
        outs[d][0:128, :] = buf[lax.rem(me[0] + d, 8)]
        outs[d][128:192, :] = slots[...]


def normal_kernel(slots, out, hot_a, hot_b, terms_a, terms_b):
    cells = lax.broadcasted_iota(jnp.int32, (128, 128), 0).astype(F32).astype(BF)
    zero = jnp.zeros((128, 128), BF)
    one = jnp.ones((128, 128), BF)

    def place(*picks):
        out = zero
        for e, x in picks:
            out = jnp.where(e, jnp.broadcast_to(x.astype(BF), (128, 128)), out)
        return out

    def build(step, hot, terms):
        group, first = lax.div(step, 4), lax.rem(step, 2) * 32
        side = pl.ds(pl.multiple_of(lax.div(lax.rem(step, 4), 2) * 128, 128), 128)
        for c in range(2):
            rows = slots[group, pl.ds(pl.multiple_of(first + 16 * c, 16), 16), side].astype(F32)
            for h in range(2):
                t = rows[8 * h : 8 * h + 8]
                w0, w1, w2, w3, v = (t[j : j + 1] for j in range(5))
                rel = cells - jnp.broadcast_to(t[6:7].astype(BF), (128, 128))
                e0, e1, e2, e3 = rel == 0, rel == 1, rel == 16, rel == 17
                parts = (
                    place((e0, w0 * w0), (e1, w1 * w1), (e2, w2 * w2), (e3, w3 * w3)),
                    place((e0, w0 * w1), (e2, w2 * w3)),
                    place((e1, w1 * w2)),
                    place((e0, w0 * w2), (e1, w1 * w3)),
                    place((e0, w0 * w3)),
                    place((e0, v * w0), (e1, v * w1), (e2, v * w2), (e3, v * w3)),
                )
                at = slice(256 * c + 128 * h, 256 * c + 128 * h + 128)
                patch = jnp.broadcast_to(t[5:6].astype(BF), (128, 128))
                hot[:, at] = jnp.where(cells == patch, one, zero)
                for j, part in enumerate(parts):
                    terms[128 * j : 128 * j + 128, at] = part

    def add(hot, terms):
        out[...] += lax.dot_general(hot[...], terms[...], NT, preferred_element_type=F32)

    out[...] = jnp.zeros(out.shape, F32)
    build(jnp.int32(0), hot_a, terms_a)

    def two(i, _):
        add(hot_a, terms_a)
        build(2 * i + 1, hot_b, terms_b)
        add(hot_b, terms_b)
        build(2 * i + 2, hot_a, terms_a)
        return 0

    lax.fori_loop(0, 15, two, 0)
    add(hot_a, terms_a)
    build(jnp.int32(31), hot_b, terms_b)
    add(hot_b, terms_b)


def resid_kernel(x, gain, *refs):
    got, (resid, scaled, slots) = refs[:8], refs[8:]
    total = x[...].astype(F32)
    for d in range(8):
        total += got[d][0:128, :].astype(F32)
        slots[d] = got[d][128:192, :]
    resid[...] = total
    out = (total * gain[...]).astype(BF)
    for k in range(8):
        scaled[k] = out


def ffn_kernel(me, core, got, *refs):
    own, far, mine, theirs = refs[0], refs[1], refs[2:5], refs[5:8]
    up, down, resid, own_dec, out, shared, sem = refs[8:]
    near, across, opposite = groups_of(me, core)
    pairs = [(own, shared.at[me[0]]), (far, shared.at[opposite])]
    for k in range(3):
        pairs.append((mine[k], shared.at[near[k]]))
        pairs.append((theirs[k], shared.at[across[k]]))
    fetch(pairs, sem)
    squares = jnp.zeros((128, 1), F32)
    for k in range(8):
        g = shared[k, 128:144, :].astype(F32)
        a = got[k].astype(F32) / (g[0:1] + g[1:2] + g[2:3])
        squares += jnp.sum(a * a, axis=1, keepdims=True)
    scale = lax.rsqrt(squares / D + EPS)
    wide = jnp.concatenate([got[k] for k in range(8)], axis=1)
    hidden = []
    for i in range(4):
        pre = jnp.dot(wide, up[:, 256 * i : 256 * i + 256], preferred_element_type=F32) * scale
        act = 0.5 * pre * (1.0 + jnp.tanh(GELU * (pre + 0.044715 * (pre * pre * pre))))
        hidden.append(act.astype(BF))
    hidden = jnp.concatenate(hidden, axis=1)
    decoded = jnp.dot(resid[...].astype(BF), own_dec[...], preferred_element_type=F32)
    for z in range(8):
        at = slice(256 * z, 256 * z + 256)
        part = jnp.dot(hidden, down[:, at], preferred_element_type=F32).astype(BF)
        out[z, :, 0:256] = part
        for i in range(2):
            side = slice(128 * i, 128 * i + 128)
            decoded += jnp.dot(part[:, side], shared[z, 0:128, side], preferred_element_type=F32)
    decoded = decoded.astype(BF)
    for z in range(8):
        out[z, :, 256:384] = decoded


def final_kernel(got, resid, normal, own_dec, state, guidance):
    total = resid[...]
    decoded = jnp.zeros((128, 128), F32)
    for k in range(8):
        total += got[k, :, 0:256].astype(F32)
        decoded += got[k, :, 256:384].astype(F32)
    state[...] = total.astype(BF)
    grad = normal[:, 0:128] * decoded - normal[:, 640:768]
    for i, d in enumerate(STEPS):
        if i:
            a = normal[:, 128 * i : 128 * i + 128]
            grad += a * pltpu.roll(decoded, 128 - d, 1) + pltpu.roll(a * decoded, d, 1)
    guidance[...] = lax.dot_general(
        grad,
        own_dec[...].astype(F32),
        NT,
        precision=lax.Precision.HIGHEST,
        preferred_element_type=F32,
    )


def stay(x):
    return pltpu.with_memory_space_constraint(x, pltpu.HBM)


def sds(shape, dtype=BF):
    return jax.ShapeDtypeStruct(shape, dtype)


def body(
    states,
    w_qkv,
    w_out,
    w_up,
    w_down,
    w_dec,
    gain_attn,
    gain_mlp,
    obs_patch,
    obs_base,
    obs_count,
    obs_weight,
    obs_value,
):
    n_tok, n_mlp = 32, 8
    x = states.reshape(128, 256)
    me = lax.axis_index("mlp").astype(jnp.int32).reshape(1)
    core = lax.rem(lax.axis_index("tok"), 2).astype(jnp.int32).reshape(1)
    pairs = [(i, i ^ 1) for i in range(n_tok)]
    chips = [[2 * i + c for i in range(16)] for c in range(2)]
    order = (1, 7, 2, 6, 3, 5, 4)
    ring = [[(i, (i + d) % n_mlp) for i in range(n_mlp)] for d in range(n_mlp)]
    vmem = pl.BlockSpec(memory_space=pltpu.VMEM)
    hbm = pl.BlockSpec(memory_space=pltpu.HBM)
    smem = pl.BlockSpec(memory_space=pltpu.SMEM)
    whole = lambda *shape: pl.BlockSpec(shape, lambda i: (0,) * len(shape))

    send = pl.pallas_call(
        pack_kernel,
        in_specs=[hbm] * 7,
        out_specs=hbm,
        out_shape=pltpu.HBM((32, 272, 128), BF),
        scratch_shapes=[
            pltpu.VMEM((64, 768), BF),
            pltpu.VMEM((64, 256), BF),
            pltpu.VMEM((1, 32, 64), jnp.int32),
            pltpu.VMEM((1, 32, 64), jnp.int32),
            pltpu.VMEM((1, 32, 4, 64), F32),
            pltpu.VMEM((1, 32, 64), F32),
            pltpu.VMEM((2, 256, 128), BF),
            pltpu.VMEM((32, 16, 128), BF),
            pltpu.SMEM((1, 32), jnp.int32),
            pltpu.SemaphoreType.DMA((40,)),
        ],
        compiler_params=params(8),
    )(*map(stay, (w_qkv, w_out.T, obs_patch, obs_base, obs_weight, obs_value, obs_count)))

    weights_in = lax.all_to_all(send, "tok", 0, 0, tiled=True)

    def shifted(k):
        return [
            (t * n_mlp + z, t * n_mlp + (z + (k if t % 2 == 0 else -k)) % n_mlp)
            for t in range(n_tok)
            for z in range(n_mlp)
        ]

    def gathered(near, far):
        mine = [lax.ppermute(near, ("tok", "mlp"), shifted(k)) for k in (1, 2, 3)]
        far_in = lax.ppermute(far, "mlp", ring[4])
        theirs = [lax.ppermute(r, "tok", pairs) for r in mine]
        return far_in, mine, theirs

    other = lax.ppermute(x, "tok", pairs)
    both, first, _ = lax.optimization_barrier((jnp.concatenate([x, other], axis=0), x, send))
    far_in, mine, theirs = gathered(both, first)
    normed = pl.pallas_call(
        norm_kernel,
        in_specs=[smem] * 2 + [hbm] * 10 + [vmem],
        out_shape=sds((8, 256, 256)),
        scratch_shapes=[pltpu.VMEM((8, 256, 256), BF), pltpu.SemaphoreType.DMA((13,))],
        compiler_params=params(8),
    )(
        me,
        core,
        *map(stay, (x, other, far_in, lax.ppermute(far_in, "tok", pairs), *mine, *theirs)),
        gain_attn.reshape(8, 1, 256),
    )
    shared = pl.pallas_call(
        shared_kernel,
        in_specs=[hbm] * 2,
        out_specs=hbm,
        out_shape=pltpu.HBM((144, 256), BF),
        scratch_shapes=[
            pltpu.VMEM((256, 128), BF),
            pltpu.VMEM((1, 256), F32),
            pltpu.VMEM((144, 256), BF),
            pltpu.SemaphoreType.DMA((2,)),
        ],
        compiler_params=params(4),
    )(stay(w_dec), stay(gain_mlp.reshape(1, 256)))
    shared, _ = lax.optimization_barrier((shared, both))
    far_shared, mine_shared, theirs_shared = gathered(shared, shared)
    weights_in, *others = lax.optimization_barrier(
        (weights_in, far_shared, *mine_shared, *theirs_shared)
    )

    qkv, slots = pl.pallas_call(
        qkv_kernel,
        out_shape=(sds((16, 48, 128)), sds((64, 256))),
        compiler_params=params(8),
    )(normed, weights_in)
    qkv_in = lax.all_to_all(qkv, "tok", 0, 0, tiled=True, axis_index_groups=chips)
    half_out, _ = lax.optimization_barrier((weights_in, qkv))
    half_out = lax.ppermute(half_out[:, 192:256, :], "tok", pairs)

    attended = pl.pallas_call(
        attend_kernel,
        in_specs=[smem, vmem],
        out_shape=sds((16, 2, 16, 128)),
        compiler_params=params(8),
    )(core, qkv_in)
    back = lax.all_to_all(attended.reshape(32, 16, 128), "tok", 0, 0, tiled=True)
    back, half_out = lax.optimization_barrier((back, half_out))

    shares = pl.pallas_call(
        share_kernel,
        grid=(1,),
        in_specs=[
            smem,
            smem,
            whole(8, 2, 2, 16, 128),
            pl.BlockSpec((32, 64, 128), lambda i: (0, 3, 0)),
            whole(32, 64, 128),
            whole(64, 256),
        ],
        out_specs=[whole(192, 256)] * 8,
        out_shape=[sds((192, 256))] * 8,
        scratch_shapes=[pltpu.VMEM((8, 128, 256), BF)],
        compiler_params=params(8),
    )(me, core, back.reshape(8, 2, 2, 16, 128), weights_in, half_out, slots)
    shares_in = [shares[0]] + [lax.ppermute(shares[d], "mlp", ring[d]) for d in order]

    resid, scaled, slots_in = pl.pallas_call(
        resid_kernel,
        out_shape=(sds((128, 256), F32), sds((8, 128, 256)), sds((8, 64, 256))),
        compiler_params=params(8),
    )(x, gain_mlp.reshape(1, 256), *shares_in)
    wide = lax.all_to_all(scaled, "mlp", 0, 0, tiled=True)

    down_out = pl.pallas_call(
        ffn_kernel,
        in_specs=[smem] * 2 + [vmem] + [hbm] * 8 + [vmem] * 4,
        out_shape=sds((8, 128, 384)),
        scratch_shapes=[
            pltpu.VMEM((8, 144, 256), BF),
            pltpu.SemaphoreType.DMA((8,)),
        ],
        compiler_params=params(8),
    )(
        me,
        core,
        wide,
        *map(stay, (shared, *others)),
        w_up,
        w_down,
        resid,
        w_dec,
    )
    down_in = lax.all_to_all(down_out, "mlp", 0, 0, tiled=True)

    slots, _ = lax.optimization_barrier((slots_in, down_out))
    normal = pl.pallas_call(
        normal_kernel,
        grid=(1,),
        in_specs=[whole(8, 64, 256)],
        out_specs=whole(128, 768),
        out_shape=sds((128, 768), F32),
        scratch_shapes=[pltpu.VMEM((128, 512), BF)] * 2 + [pltpu.VMEM((768, 512), BF)] * 2,
        compiler_params=params(8),
        cost_estimate=pl.CostEstimate(
            flops=4_000_000_000, bytes_accessed=1_000_000, transcendentals=0
        ),
    )(slots)
    down_in, normal = lax.optimization_barrier((down_in, normal))

    state, guidance = pl.pallas_call(
        final_kernel,
        out_shape=(sds((128, 256)), sds((128, 256), F32)),
        compiler_params=params(8),
    )(down_in, resid, normal, w_dec)
    return state.reshape(8, 16, 256), guidance.reshape(8, 16, 256)


def solution(mesh):
    placed = (
        P(None, "tok", "mlp"),
        P("tok", "mlp"),
        P("mlp", "tok"),
        P(None, "mlp"),
        P("mlp", None),
        P("mlp", None),
        P(),
        P("mlp"),
        P(("tok", "mlp"), None, None),
        P(("tok", "mlp"), None, None),
        P(("tok", "mlp"), None),
        P(("tok", "mlp"), None, None, None),
        P(("tok", "mlp"), None, None),
    )
    return jax.shard_map(
        body,
        mesh=mesh,
        in_specs=placed,
        out_specs=(P(None, "tok", "mlp"), P(None, "tok", "mlp")),
        check_vma=False,
    )
```

```python
import functools

import jax
import jax.numpy as jnp
from jax import lax
from jax.experimental import pallas as pl
from jax.experimental.pallas import tpu as pltpu
from jax.sharding import PartitionSpec as P

D = 2048
HD = 64
EPS = 1e-06
BF = jnp.bfloat16
F32 = jnp.float32
NT = (((1,), (1,)), ((), ()))
GELU = 0.7978845608028654
STEPS = (0, 1, 15, 16, 17)


def params(mib):
    return pltpu.CompilerParams(vmem_limit_bytes=mib * 1024 * 1024)


def lanes(shape):
    return lax.broadcasted_iota(jnp.int32, shape, len(shape) - 1)


def half(x):
    return pltpu.roll(x, 64, 1)


def left(shape):
    return lanes(shape) < 64


def fetch(pairs, sem):
    copies = [pltpu.make_async_copy(src, dst, sem.at[i]) for i, (src, dst) in enumerate(pairs)]
    for copy in copies:
        copy.start()
    for copy in copies:
        copy.wait()


def pack_kernel(core, *refs):
    ins, (out, both, far), bufs = refs[:11], refs[11:14], refs[14:22]
    counts, w_buf, g_buf, both_buf, far_buf, sem = refs[22:]
    wqkv, wout_t, patch, base, weight, value, blocks, obs = bufs
    dests = [*bufs[:6], counts, w_buf, g_buf]
    dests += [both_buf.at[pl.ds(0, 128), :]]
    loads = [pltpu.make_async_copy(ins[i], dests[i], sem.at[i]) for i in range(10)]
    loads.append(pltpu.make_async_copy(ins[9], far_buf.at[pl.ds(0, 128), :], sem.at[10]))
    for load in loads:
        load.start()
    loads[0].wait()
    loads[1].wait()
    for c in range(2):
        for j in range(3):
            blocks[c, 64 * j : 64 * j + 64, :] = wqkv[:, 256 * j + 128 * c : 256 * j + 128 * c + 128]
        blocks[c, 192:256, :] = wout_t[:, 128 * c : 128 * c + 128]
    n = out.shape[0]
    copies = [
        pltpu.make_async_copy(blocks.at[d % 2], out.at[d, pl.ds(0, 256), :], sem.at[12 + d])
        for d in range(n)
    ]
    for copy in copies:
        copy.start()
    for load in loads[2:]:
        load.wait()
    g = g_buf[...]
    high = g.astype(BF).astype(F32)
    mid = (g - high).astype(BF).astype(F32)
    rows = jnp.concatenate([high, mid, g - high - mid, jnp.zeros((13, 256), F32)], axis=0)
    both_buf[128:256, :] = ins[10][...]
    both_buf[256:384, 0:128] = w_buf[0:128, :]
    both_buf[256:384, 128:256] = w_buf[128:256, :]
    both_buf[384:400, :] = rows.astype(BF)
    both_buf[400:416, :] = jnp.zeros((16, 256), BF)
    far_buf[128:208, :] = both_buf[pl.ds(pl.multiple_of(256 + 80 * core[0], 16), 80), :]
    more = [
        pltpu.make_async_copy(both_buf, both, sem.at[13 + n]),
        pltpu.make_async_copy(far_buf, far, sem.at[14 + n]),
    ]
    for copy in more:
        copy.start()
    copies += more
    slots = lanes((4, 64))
    zero = jnp.zeros((1, 64), F32)
    rest = jnp.zeros((12, 128), F32)
    for dest in range(n):
        row = slice(dest, dest + 1)
        live = slots < counts[0, dest]
        w = jnp.where(live, weight[0, dest], 0.0)
        v = jnp.where(live[0:1], value[0, row, :], 0.0)
        other = [v, patch[0, row, :].astype(F32), base[0, row, :].astype(F32), zero]
        both = jnp.concatenate([w, jnp.concatenate(other, axis=0)], axis=1)
        obs[dest] = jnp.concatenate([both, rest], axis=0).astype(BF)
    last = pltpu.make_async_copy(obs, out.at[:, pl.ds(256, 16), :], sem.at[12 + n])
    last.start()
    for copy in copies:
        copy.wait()
    last.wait()


def groups_of(me, core):
    turn = 1 - 2 * core[0]
    mine = [lax.rem(me[0] - turn * k + 8, 8) for k in (1, 2, 3)]
    theirs = [lax.rem(me[0] + turn * k + 8, 8) for k in (1, 2, 3)]
    return mine, theirs, lax.rem(me[0] + 4, 8)


def norm_kernel(me, core, *refs):
    both, far, far_sib, mine, theirs = *refs[:3], refs[3:6], refs[6:9]
    gain, out, buf, sem = refs[9:]
    near, across, opposite = groups_of(me, core)
    low, top = pl.ds(0, 128), pl.ds(128, 128)
    pairs = [
        (both.at[pl.ds(0, 256), :], buf.at[me[0]]),
        (far.at[low, :], buf.at[opposite, low, :]),
        (far_sib.at[low, :], buf.at[opposite, top, :]),
    ]
    for k in range(3):
        pairs.append((mine[k].at[pl.ds(0, 256), :], buf.at[near[k]]))
        pairs.append((theirs[k].at[top, :], buf.at[across[k], low, :]))
        pairs.append((theirs[k].at[low, :], buf.at[across[k], top, :]))
    fetch(pairs, sem)
    squares = jnp.zeros((256, 1), F32)
    for k in range(8):
        a = buf[k].astype(F32)
        squares += jnp.sum(a * a, axis=1, keepdims=True)
    r = lax.rsqrt(squares / D + EPS)
    for k in range(8):
        out[k] = (buf[k].astype(F32) * r * gain[k]).astype(BF)


def qkv_kernel(normed, w, out, slots):
    acc = jnp.zeros((256, 384), F32)
    for k in range(8):
        cols = [w[4 * k : 4 * k + 4, 64 * j : 64 * j + 64, :].reshape(256, 128) for j in range(3)]
        acc += jnp.dot(normed[k], jnp.concatenate(cols, axis=1), preferred_element_type=F32)
    q, k, v = acc[:, 0:128], acc[:, 128:256], acc[:, 256:384]
    low = left((256, 128))
    pairs = (jnp.where(low, q, half(k)), jnp.where(low, half(q), k))
    own, sib = v[0:128], v[128:256]
    low = left((128, 128))
    values = (jnp.where(low, own, half(sib)), jnp.where(low, half(own), sib))
    for g in range(2):
        qk = pairs[g].astype(BF)
        vv = values[g].astype(BF)
        for s in range(8):
            out[2 * s + g, 0:16, :] = qk[16 * s : 16 * s + 16, :]
            out[2 * s + g, 16:32, :] = qk[128 + 16 * s : 144 + 16 * s, :]
            out[2 * s + g, 32:48, :] = vv[16 * s : 16 * s + 16, :]
    low = left((16, 128))
    tiles = []
    for pair in range(16):
        a = w[2 * pair, 256:272, :].astype(F32)
        b = w[2 * pair + 1, 256:272, :].astype(F32)
        tiles.append(jnp.where(low, a, half(b))[0:4])
        tiles.append(jnp.where(low, half(a), b)[0:4])
    slots[:, 0:128] = jnp.concatenate(tiles[:16], axis=0).astype(BF)
    slots[:, 128:256] = jnp.concatenate(tiles[16:], axis=0).astype(BF)


def attend_kernel(core, got, out):
    qk_own = got[:, 0:16, :].reshape(256, 128)
    qk_sib = got[:, 16:32, :].reshape(256, 128)
    vv = got[:, 32:48, :].reshape(256, 128)
    low = left((256, 128))

    def mix(qk):
        query = (jnp.where(low, 0.0, half(qk.astype(F32))) * (1.0 / HD**0.5)).astype(BF)
        first = lax.dot_general(query, qk_own, NT, preferred_element_type=F32)
        second = lax.dot_general(query, qk_sib, NT, preferred_element_type=F32)
        top = jnp.maximum(
            jnp.max(first, axis=1, keepdims=True), jnp.max(second, axis=1, keepdims=True)
        )
        first = jnp.exp(first - top)
        second = jnp.exp(second - top)
        total = jnp.sum(first, axis=1, keepdims=True) + jnp.sum(second, axis=1, keepdims=True)
        one = jnp.dot(first.astype(BF), vv, preferred_element_type=F32)
        two = jnp.dot(second.astype(BF), vv, preferred_element_type=F32)
        return (one + half(two)) / total

    c = core[0]
    out[:, c] = mix(qk_own).astype(BF).reshape(16, 16, 128)
    out[:, 1 - c] = mix(qk_sib).astype(BF).reshape(16, 16, 128)


def share_kernel(me, core, got, w, w_sib, slots, *refs):
    outs, buf = refs[:8], refs[8]
    low = left((128, 128))

    def heads_of(c):
        a = got[:, 0, c].reshape(128, 128).astype(F32)
        b = got[:, 1, c].reshape(128, 128).astype(F32)
        return jnp.where(low, a, half(b)).astype(BF)

    own, other = heads_of(core[0]), heads_of(1 - core[0])
    for z in range(8):
        at = slice(4 * z, 4 * z + 4)
        part = lax.dot_general(own, w[at].reshape(256, 128), NT, preferred_element_type=F32)
        part += lax.dot_general(other, w_sib[at].reshape(256, 128), NT, preferred_element_type=F32)
        buf[z] = part.astype(BF)
    for d in range(8):
        outs[d][0:128, :] = buf[lax.rem(me[0] + d, 8)]
        outs[d][128:192, :] = slots[...]


def normal_kernel(slots, out, hot_a, hot_b, terms_a, terms_b):
    cells = lax.broadcasted_iota(jnp.int32, (128, 128), 0).astype(F32).astype(BF)
    zero = jnp.zeros((128, 128), BF)
    one = jnp.ones((128, 128), BF)

    def place(*picks):
        out = zero
        for e, x in picks:
            out = jnp.where(e, jnp.broadcast_to(x.astype(BF), (128, 128)), out)
        return out

    def build(step, hot, terms):
        group, first = lax.div(step, 4), lax.rem(step, 2) * 32
        side = pl.ds(pl.multiple_of(lax.div(lax.rem(step, 4), 2) * 128, 128), 128)
        for c in range(2):
            rows = slots[group, pl.ds(pl.multiple_of(first + 16 * c, 16), 16), side].astype(F32)
            for h in range(2):
                t = rows[8 * h : 8 * h + 8]
                w0, w1, w2, w3, v = (t[j : j + 1] for j in range(5))
                rel = cells - jnp.broadcast_to(t[6:7].astype(BF), (128, 128))
                e0, e1, e2, e3 = rel == 0, rel == 1, rel == 16, rel == 17
                parts = (
                    place((e0, w0 * w0), (e1, w1 * w1), (e2, w2 * w2), (e3, w3 * w3)),
                    place((e0, w0 * w1), (e2, w2 * w3)),
                    place((e1, w1 * w2)),
                    place((e0, w0 * w2), (e1, w1 * w3)),
                    place((e0, w0 * w3)),
                    place((e0, v * w0), (e1, v * w1), (e2, v * w2), (e3, v * w3)),
                )
                at = slice(256 * c + 128 * h, 256 * c + 128 * h + 128)
                patch = jnp.broadcast_to(t[5:6].astype(BF), (128, 128))
                hot[:, at] = jnp.where(cells == patch, one, zero)
                for j, part in enumerate(parts):
                    terms[128 * j : 128 * j + 128, at] = part

    def add(hot, terms):
        out[...] += lax.dot_general(hot[...], terms[...], NT, preferred_element_type=F32)

    out[...] = jnp.zeros(out.shape, F32)
    build(jnp.int32(0), hot_a, terms_a)

    def two(i, _):
        add(hot_a, terms_a)
        build(2 * i + 1, hot_b, terms_b)
        add(hot_b, terms_b)
        build(2 * i + 2, hot_a, terms_a)
        return 0

    lax.fori_loop(0, 15, two, 0)
    add(hot_a, terms_a)
    build(jnp.int32(31), hot_b, terms_b)
    add(hot_b, terms_b)


def resid_kernel(x, gain, *refs):
    got, (resid, scaled, slots) = refs[:8], refs[8:]
    total = x[...].astype(F32)
    for d in range(8):
        total += got[d][0:128, :].astype(F32)
        slots[d] = got[d][128:192, :]
    resid[...] = total
    out = (total * gain[...]).astype(BF)
    for k in range(8):
        scaled[k] = out


def ffn_kernel(me, core, got, *refs):
    own, far, far_sib, mine, theirs = refs[0], refs[1], refs[2], refs[3:6], refs[6:9]
    up, down, resid, own_dec, out, shared, sem = refs[9:]
    near, across, opposite = groups_of(me, core)
    common = pl.ds(256, 160)
    pairs = [(own.at[common, :], shared.at[me[0]])]
    for half_far, c in ((far, core[0]), (far_sib, 1 - core[0])):
        side = pl.ds(pl.multiple_of(80 * c, 16), 80)
        pairs.append((half_far.at[pl.ds(128, 80), :], shared.at[opposite, side, :]))
    for k in range(3):
        pairs.append((mine[k].at[common, :], shared.at[near[k]]))
        pairs.append((theirs[k].at[common, :], shared.at[across[k]]))
    fetch(pairs, sem)
    squares = jnp.zeros((128, 1), F32)
    for k in range(8):
        g = shared[k, 128:144, :].astype(F32)
        a = got[k].astype(F32) / (g[0:1] + g[1:2] + g[2:3])
        squares += jnp.sum(a * a, axis=1, keepdims=True)
    scale = lax.rsqrt(squares / D + EPS)
    wide = jnp.concatenate([got[k] for k in range(8)], axis=1)
    hidden = []
    for i in range(4):
        pre = jnp.dot(wide, up[:, 256 * i : 256 * i + 256], preferred_element_type=F32) * scale
        act = 0.5 * pre * (1.0 + jnp.tanh(GELU * (pre + 0.044715 * (pre * pre * pre))))
        hidden.append(act.astype(BF))
    hidden = jnp.concatenate(hidden, axis=1)
    decoded = jnp.dot(resid[...].astype(BF), own_dec[...], preferred_element_type=F32)
    for z in range(8):
        at = slice(256 * z, 256 * z + 256)
        part = jnp.dot(hidden, down[:, at], preferred_element_type=F32).astype(BF)
        out[z, :, 0:256] = part
        for i in range(2):
            side = slice(128 * i, 128 * i + 128)
            decoded += jnp.dot(part[:, side], shared[z, 0:128, side], preferred_element_type=F32)
    decoded = decoded.astype(BF)
    for z in range(8):
        out[z, :, 256:384] = decoded


def final_kernel(got, resid, normal, own_dec, state, guidance):
    total = resid[...]
    decoded = jnp.zeros((128, 128), F32)
    for k in range(8):
        total += got[k, :, 0:256].astype(F32)
        decoded += got[k, :, 256:384].astype(F32)
    state[...] = total.astype(BF)
    grad = normal[:, 0:128] * decoded - normal[:, 640:768]
    for i, d in enumerate(STEPS):
        if i:
            a = normal[:, 128 * i : 128 * i + 128]
            grad += a * pltpu.roll(decoded, 128 - d, 1) + pltpu.roll(a * decoded, d, 1)
    guidance[...] = lax.dot_general(
        grad,
        own_dec[...].astype(F32),
        NT,
        precision=lax.Precision.HIGHEST,
        preferred_element_type=F32,
    )


def stay(x):
    return pltpu.with_memory_space_constraint(x, pltpu.HBM)


def sds(shape, dtype=BF):
    return jax.ShapeDtypeStruct(shape, dtype)


def body(
    states,
    w_qkv,
    w_out,
    w_up,
    w_down,
    w_dec,
    gain_attn,
    gain_mlp,
    obs_patch,
    obs_base,
    obs_count,
    obs_weight,
    obs_value,
):
    n_tok, n_mlp = 32, 8
    x = states.reshape(128, 256)
    me = lax.axis_index("mlp").astype(jnp.int32).reshape(1)
    core = lax.rem(lax.axis_index("tok"), 2).astype(jnp.int32).reshape(1)
    pairs = [(i, i ^ 1) for i in range(n_tok)]
    chips = [[2 * i + c for i in range(16)] for c in range(2)]
    order = (1, 7, 2, 6, 3, 5, 4)
    ring = [[(i, (i + d) % n_mlp) for i in range(n_mlp)] for d in range(n_mlp)]
    vmem = pl.BlockSpec(memory_space=pltpu.VMEM)
    hbm = pl.BlockSpec(memory_space=pltpu.HBM)
    smem = pl.BlockSpec(memory_space=pltpu.SMEM)
    whole = lambda *shape: pl.BlockSpec(shape, lambda i: (0,) * len(shape))

    other = lax.ppermute(x, "tok", pairs)
    send, both, far = pl.pallas_call(
        pack_kernel,
        in_specs=[smem] + [hbm] * 10 + [vmem],
        out_specs=(hbm, hbm, hbm),
        out_shape=(
            pltpu.HBM((32, 272, 128), BF),
            pltpu.HBM((416, 256), BF),
            pltpu.HBM((208, 256), BF),
        ),
        scratch_shapes=[
            pltpu.VMEM((64, 768), BF),
            pltpu.VMEM((64, 256), BF),
            pltpu.VMEM((1, 32, 64), jnp.int32),
            pltpu.VMEM((1, 32, 64), jnp.int32),
            pltpu.VMEM((1, 32, 4, 64), F32),
            pltpu.VMEM((1, 32, 64), F32),
            pltpu.VMEM((2, 256, 128), BF),
            pltpu.VMEM((32, 16, 128), BF),
            pltpu.SMEM((1, 32), jnp.int32),
            pltpu.VMEM((256, 128), BF),
            pltpu.VMEM((1, 256), F32),
            pltpu.VMEM((416, 256), BF),
            pltpu.VMEM((208, 256), BF),
            pltpu.SemaphoreType.DMA((47,)),
        ],
        compiler_params=params(8),
    )(
        core,
        *map(stay, (w_qkv, w_out.T, obs_patch, obs_base, obs_weight, obs_value, obs_count)),
        stay(w_dec),
        stay(gain_mlp.reshape(1, 256)),
        stay(x),
        other,
    )


    def shifted(k):
        return [
            (t * n_mlp + z, t * n_mlp + (z + (k if t % 2 == 0 else -k)) % n_mlp)
            for t in range(n_tok)
            for z in range(n_mlp)
        ]

    def gathered(near, far):
        mine = [lax.ppermute(near, ("tok", "mlp"), shifted(k)) for k in (1, 2, 3)]
        far_in = lax.ppermute(far, "mlp", ring[4])
        theirs = [lax.ppermute(r, "tok", pairs) for r in mine]
        return far_in, mine, theirs

    weights_in = lax.all_to_all(send, "tok", 0, 0, tiled=True)
    far_in, mine, theirs = gathered(both, far)
    packs = (both, far_in, lax.ppermute(far_in, "tok", pairs), *mine, *theirs)
    normed = pl.pallas_call(
        norm_kernel,
        in_specs=[smem] * 2 + [hbm] * 9 + [vmem],
        out_shape=sds((8, 256, 256)),
        scratch_shapes=[pltpu.VMEM((8, 256, 256), BF), pltpu.SemaphoreType.DMA((13,))],
        compiler_params=params(8),
    )(
        me,
        core,
        *map(stay, packs),
        gain_attn.reshape(8, 1, 256),
    )
    qkv, slots = pl.pallas_call(
        qkv_kernel,
        out_shape=(sds((16, 48, 128)), sds((64, 256))),
        compiler_params=params(8),
    )(normed, weights_in)
    qkv_in = lax.all_to_all(qkv, "tok", 0, 0, tiled=True, axis_index_groups=chips)
    half_out, _ = lax.optimization_barrier((weights_in, qkv))
    half_out = lax.ppermute(half_out[:, 192:256, :], "tok", pairs)

    attended = pl.pallas_call(
        attend_kernel,
        in_specs=[smem, vmem],
        out_shape=sds((16, 2, 16, 128)),
        compiler_params=params(8),
    )(core, qkv_in)
    back = lax.all_to_all(attended.reshape(32, 16, 128), "tok", 0, 0, tiled=True)
    back, half_out = lax.optimization_barrier((back, half_out))

    shares = pl.pallas_call(
        share_kernel,
        grid=(1,),
        in_specs=[
            smem,
            smem,
            whole(8, 2, 2, 16, 128),
            pl.BlockSpec((32, 64, 128), lambda i: (0, 3, 0)),
            whole(32, 64, 128),
            whole(64, 256),
        ],
        out_specs=[whole(192, 256)] * 8,
        out_shape=[sds((192, 256))] * 8,
        scratch_shapes=[pltpu.VMEM((8, 128, 256), BF)],
        compiler_params=params(8),
    )(me, core, back.reshape(8, 2, 2, 16, 128), weights_in, half_out, slots)
    shares_in = [shares[0]] + [lax.ppermute(shares[d], "mlp", ring[d]) for d in order]

    resid, scaled, slots_in = pl.pallas_call(
        resid_kernel,
        out_shape=(sds((128, 256), F32), sds((8, 128, 256)), sds((8, 64, 256))),
        compiler_params=params(8),
    )(x, gain_mlp.reshape(1, 256), *shares_in)
    wide = lax.all_to_all(scaled, "mlp", 0, 0, tiled=True)

    down_out = pl.pallas_call(
        ffn_kernel,
        in_specs=[smem] * 2 + [vmem] + [hbm] * 9 + [vmem] * 4,
        out_shape=sds((8, 128, 384)),
        scratch_shapes=[
            pltpu.VMEM((8, 160, 256), BF),
            pltpu.SemaphoreType.DMA((9,)),
        ],
        compiler_params=params(8),
    )(
        me,
        core,
        wide,
        *map(stay, packs),
        w_up,
        w_down,
        resid,
        w_dec,
    )
    down_in = lax.all_to_all(down_out, "mlp", 0, 0, tiled=True)

    slots, _ = lax.optimization_barrier((slots_in, down_out))
    normal = pl.pallas_call(
        normal_kernel,
        grid=(1,),
        in_specs=[whole(8, 64, 256)],
        out_specs=whole(128, 768),
        out_shape=sds((128, 768), F32),
        scratch_shapes=[pltpu.VMEM((128, 512), BF)] * 2 + [pltpu.VMEM((768, 512), BF)] * 2,
        compiler_params=params(8),
        cost_estimate=pl.CostEstimate(
            flops=4_000_000_000, bytes_accessed=1_000_000, transcendentals=0
        ),
    )(slots)
    down_in, normal = lax.optimization_barrier((down_in, normal))

    state, guidance = pl.pallas_call(
        final_kernel,
        out_shape=(sds((128, 256)), sds((128, 256), F32)),
        compiler_params=params(8),
    )(down_in, resid, normal, w_dec)
    return state.reshape(8, 16, 256), guidance.reshape(8, 16, 256)


def solution(mesh):
    placed = (
        P(None, "tok", "mlp"),
        P("tok", "mlp"),
        P("mlp", "tok"),
        P(None, "mlp"),
        P("mlp", None),
        P("mlp", None),
        P(),
        P("mlp"),
        P(("tok", "mlp"), None, None),
        P(("tok", "mlp"), None, None),
        P(("tok", "mlp"), None),
        P(("tok", "mlp"), None, None, None),
        P(("tok", "mlp"), None, None),
    )
    return jax.shard_map(
        body,
        mesh=mesh,
        in_specs=placed,
        out_specs=(P(None, "tok", "mlp"), P(None, "tok", "mlp")),
        check_vma=False,
    )
```

```python
import functools

import jax
import jax.numpy as jnp
from jax import lax
from jax.experimental import pallas as pl
from jax.experimental.pallas import tpu as pltpu
from jax.sharding import PartitionSpec as P

D = 2048
HD = 64
EPS = 1e-06
BF = jnp.bfloat16
F32 = jnp.float32
NT = (((1,), (1,)), ((), ()))
GELU = 0.7978845608028654
STEPS = (0, 1, 15, 16, 17)


def params(mib):
    return pltpu.CompilerParams(vmem_limit_bytes=mib * 1024 * 1024)


def lanes(shape):
    return lax.broadcasted_iota(jnp.int32, shape, len(shape) - 1)


def half(x):
    return pltpu.roll(x, 64, 1)


def left(shape):
    return lanes(shape) < 64


def fetch(pairs, sem):
    copies = [pltpu.make_async_copy(src, dst, sem.at[i]) for i, (src, dst) in enumerate(pairs)]
    for copy in copies:
        copy.start()
    for copy in copies:
        copy.wait()


def pack_kernel(core, *refs):
    ins, (out, both, far), bufs = refs[:11], refs[11:14], refs[14:22]
    counts, w_buf, g_buf, both_buf, far_buf, sem = refs[22:]
    wqkv, wout_t, patch, base, weight, value, blocks, obs = bufs
    dests = [*bufs[:6], counts, w_buf, g_buf]
    dests += [both_buf.at[pl.ds(0, 128), :]]
    loads = [pltpu.make_async_copy(ins[i], dests[i], sem.at[i]) for i in range(10)]
    loads.append(pltpu.make_async_copy(ins[9], far_buf.at[pl.ds(0, 128), :], sem.at[10]))
    for load in loads:
        load.start()
    loads[0].wait()
    loads[1].wait()
    for c in range(2):
        for j in range(3):
            blocks[c, 64 * j : 64 * j + 64, :] = wqkv[:, 256 * j + 128 * c : 256 * j + 128 * c + 128]
        blocks[c, 192:256, :] = wout_t[:, 128 * c : 128 * c + 128]
    n = out.shape[0]
    copies = [
        pltpu.make_async_copy(blocks.at[d % 2], out.at[d, pl.ds(0, 256), :], sem.at[12 + d])
        for d in range(n)
    ]
    for copy in copies:
        copy.start()
    for load in loads[2:]:
        load.wait()
    g = g_buf[...]
    high = g.astype(BF).astype(F32)
    mid = (g - high).astype(BF).astype(F32)
    rows = jnp.concatenate([high, mid, g - high - mid, jnp.zeros((13, 256), F32)], axis=0)
    both_buf[128:256, :] = ins[10][...]
    both_buf[256:384, 0:128] = w_buf[0:128, :]
    both_buf[256:384, 128:256] = w_buf[128:256, :]
    both_buf[384:400, :] = rows.astype(BF)
    both_buf[400:416, :] = jnp.zeros((16, 256), BF)
    far_buf[128:208, :] = both_buf[pl.ds(pl.multiple_of(256 + 80 * core[0], 16), 80), :]
    more = [
        pltpu.make_async_copy(both_buf, both, sem.at[13 + n]),
        pltpu.make_async_copy(far_buf, far, sem.at[14 + n]),
    ]
    for copy in more:
        copy.start()
    copies += more
    slots = lanes((4, 64))
    zero = jnp.zeros((1, 64), F32)
    rest = jnp.zeros((12, 128), F32)
    for dest in range(n):
        row = slice(dest, dest + 1)
        live = slots < counts[0, dest]
        w = jnp.where(live, weight[0, dest], 0.0)
        v = jnp.where(live[0:1], value[0, row, :], 0.0)
        other = [v, patch[0, row, :].astype(F32), base[0, row, :].astype(F32), zero]
        both = jnp.concatenate([w, jnp.concatenate(other, axis=0)], axis=1)
        obs[dest] = jnp.concatenate([both, rest], axis=0).astype(BF)
    last = pltpu.make_async_copy(obs, out.at[:, pl.ds(256, 16), :], sem.at[12 + n])
    last.start()
    for copy in copies:
        copy.wait()
    last.wait()


def groups_of(me, core):
    turn = 1 - 2 * core[0]
    mine = [lax.rem(me[0] - turn * k + 8, 8) for k in (1, 2, 3)]
    theirs = [lax.rem(me[0] + turn * k + 8, 8) for k in (1, 2, 3)]
    return mine, theirs, lax.rem(me[0] + 4, 8)


def norm_kernel(me, core, *refs):
    both, far, far_sib, mine, theirs = *refs[:3], refs[3:6], refs[6:9]
    gain, out, buf, sem = refs[9:]
    near, across, opposite = groups_of(me, core)
    low, top = pl.ds(0, 128), pl.ds(128, 128)
    pairs = [
        (both.at[pl.ds(0, 256), :], buf.at[me[0]]),
        (far.at[low, :], buf.at[opposite, low, :]),
        (far_sib.at[low, :], buf.at[opposite, top, :]),
    ]
    for k in range(3):
        pairs.append((mine[k].at[pl.ds(0, 256), :], buf.at[near[k]]))
        pairs.append((theirs[k].at[top, :], buf.at[across[k], low, :]))
        pairs.append((theirs[k].at[low, :], buf.at[across[k], top, :]))
    fetch(pairs, sem)
    squares = jnp.zeros((256, 1), F32)
    for k in range(8):
        a = buf[k].astype(F32)
        squares += jnp.sum(a * a, axis=1, keepdims=True)
    r = lax.rsqrt(squares / D + EPS)
    for k in range(8):
        out[k] = (buf[k].astype(F32) * r * gain[k]).astype(BF)


def qkv_kernel(normed, w, out, slots):
    acc = jnp.zeros((256, 384), F32)
    for k in range(8):
        cols = [w[4 * k : 4 * k + 4, 64 * j : 64 * j + 64, :].reshape(256, 128) for j in range(3)]
        acc += jnp.dot(normed[k], jnp.concatenate(cols, axis=1), preferred_element_type=F32)
    q, k, v = acc[:, 0:128], acc[:, 128:256], acc[:, 256:384]
    low = left((256, 128))
    pairs = (jnp.where(low, q, half(k)), jnp.where(low, half(q), k))
    own, sib = v[0:128], v[128:256]
    low = left((128, 128))
    values = (jnp.where(low, own, half(sib)), jnp.where(low, half(own), sib))
    for g in range(2):
        qk = pairs[g].astype(BF)
        vv = values[g].astype(BF)
        for s in range(8):
            out[2 * s + g, 0:16, :] = qk[16 * s : 16 * s + 16, :]
            out[2 * s + g, 16:32, :] = qk[128 + 16 * s : 144 + 16 * s, :]
            out[2 * s + g, 32:48, :] = vv[16 * s : 16 * s + 16, :]
    low = left((16, 128))
    tiles = []
    for pair in range(16):
        a = w[2 * pair, 256:272, :].astype(F32)
        b = w[2 * pair + 1, 256:272, :].astype(F32)
        tiles.append(jnp.where(low, a, half(b))[0:4])
        tiles.append(jnp.where(low, half(a), b)[0:4])
    slots[:, 0:128] = jnp.concatenate(tiles[:16], axis=0).astype(BF)
    slots[:, 128:256] = jnp.concatenate(tiles[16:], axis=0).astype(BF)


def attend_kernel(core, got, out):
    qk_own = got[:, 0:16, :].reshape(256, 128)
    qk_sib = got[:, 16:32, :].reshape(256, 128)
    vv = got[:, 32:48, :].reshape(256, 128)
    low = left((256, 128))

    def mix(qk):
        query = (jnp.where(low, 0.0, half(qk.astype(F32))) * (1.0 / HD**0.5)).astype(BF)
        first = lax.dot_general(query, qk_own, NT, preferred_element_type=F32)
        second = lax.dot_general(query, qk_sib, NT, preferred_element_type=F32)
        top = jnp.maximum(
            jnp.max(first, axis=1, keepdims=True), jnp.max(second, axis=1, keepdims=True)
        )
        first = jnp.exp(first - top)
        second = jnp.exp(second - top)
        total = jnp.sum(first, axis=1, keepdims=True) + jnp.sum(second, axis=1, keepdims=True)
        one = jnp.dot(first.astype(BF), vv, preferred_element_type=F32)
        two = jnp.dot(second.astype(BF), vv, preferred_element_type=F32)
        return (one + half(two)) / total

    c = core[0]
    out[:, c] = mix(qk_own).astype(BF).reshape(16, 16, 128)
    out[:, 1 - c] = mix(qk_sib).astype(BF).reshape(16, 16, 128)


def share_kernel(me, core, got, w, w_sib, slots, *refs):
    outs, buf = refs[:8], refs[8]
    low = left((128, 128))

    def heads_of(c):
        a = got[:, 0, c].reshape(128, 128).astype(F32)
        b = got[:, 1, c].reshape(128, 128).astype(F32)
        return jnp.where(low, a, half(b)).astype(BF)

    own, other = heads_of(core[0]), heads_of(1 - core[0])
    for z in range(8):
        at = slice(4 * z, 4 * z + 4)
        part = lax.dot_general(own, w[at].reshape(256, 128), NT, preferred_element_type=F32)
        part += lax.dot_general(other, w_sib[at].reshape(256, 128), NT, preferred_element_type=F32)
        buf[z] = part.astype(BF)
    for d in range(8):
        outs[d][0:128, :] = buf[lax.rem(me[0] + d, 8)]
        outs[d][128:192, :] = slots[...]


def normal_kernel(slots, out, hot_a, hot_b, terms_a, terms_b):
    cells = lax.broadcasted_iota(jnp.int32, (128, 128), 0).astype(F32).astype(BF)
    zero = jnp.zeros((128, 128), BF)
    one = jnp.ones((128, 128), BF)

    def place(*picks):
        out = zero
        for e, x in picks:
            out = jnp.where(e, jnp.broadcast_to(x.astype(BF), (128, 128)), out)
        return out

    def build(step, hot, terms):
        group, first = lax.div(step, 4), lax.rem(step, 2) * 32
        side = pl.ds(pl.multiple_of(lax.div(lax.rem(step, 4), 2) * 128, 128), 128)
        for c in range(2):
            rows = slots[group, pl.ds(pl.multiple_of(first + 16 * c, 16), 16), side].astype(F32)
            for h in range(2):
                t = rows[8 * h : 8 * h + 8]
                w0, w1, w2, w3, v = (t[j : j + 1] for j in range(5))
                rel = cells - jnp.broadcast_to(t[6:7].astype(BF), (128, 128))
                e0, e1, e2, e3 = rel == 0, rel == 1, rel == 16, rel == 17
                parts = (
                    place((e0, w0 * w0), (e1, w1 * w1), (e2, w2 * w2), (e3, w3 * w3)),
                    place((e0, w0 * w1), (e2, w2 * w3)),
                    place((e1, w1 * w2)),
                    place((e0, w0 * w2), (e1, w1 * w3)),
                    place((e0, w0 * w3)),
                    place((e0, v * w0), (e1, v * w1), (e2, v * w2), (e3, v * w3)),
                )
                at = slice(256 * c + 128 * h, 256 * c + 128 * h + 128)
                patch = jnp.broadcast_to(t[5:6].astype(BF), (128, 128))
                hot[:, at] = jnp.where(cells == patch, one, zero)
                for j, part in enumerate(parts):
                    terms[128 * j : 128 * j + 128, at] = part

    def add(hot, terms):
        out[...] += lax.dot_general(hot[...], terms[...], NT, preferred_element_type=F32)

    out[...] = jnp.zeros(out.shape, F32)
    build(jnp.int32(0), hot_a, terms_a)

    def two(i, _):
        add(hot_a, terms_a)
        build(2 * i + 1, hot_b, terms_b)
        add(hot_b, terms_b)
        build(2 * i + 2, hot_a, terms_a)
        return 0

    lax.fori_loop(0, 15, two, 0)
    add(hot_a, terms_a)
    build(jnp.int32(31), hot_b, terms_b)
    add(hot_b, terms_b)


def resid_kernel(x, gain, *refs):
    got, (resid, scaled, slots) = refs[:8], refs[8:]
    total = x[...].astype(F32)
    for d in range(8):
        total += got[d][0:128, :].astype(F32)
        slots[d] = got[d][128:192, :]
    resid[...] = total
    out = (total * gain[...]).astype(BF)
    for k in range(8):
        scaled[k] = out


def ffn_kernel(me, core, got, *refs):
    own, far, far_sib, mine, theirs = refs[0], refs[1], refs[2], refs[3:6], refs[6:9]
    up, down, resid, own_dec, out, shared, sem = refs[9:]
    near, across, opposite = groups_of(me, core)
    common = pl.ds(256, 160)
    pairs = [(own.at[common, :], shared.at[me[0]])]
    for half_far, c in ((far, core[0]), (far_sib, 1 - core[0])):
        side = pl.ds(pl.multiple_of(80 * c, 16), 80)
        pairs.append((half_far.at[pl.ds(128, 80), :], shared.at[opposite, side, :]))
    for k in range(3):
        pairs.append((mine[k].at[common, :], shared.at[near[k]]))
        pairs.append((theirs[k].at[common, :], shared.at[across[k]]))
    fetch(pairs, sem)
    squares = jnp.zeros((128, 1), F32)
    for k in range(8):
        g = shared[k, 128:144, :].astype(F32)
        a = got[k].astype(F32) / (g[0:1] + g[1:2] + g[2:3])
        squares += jnp.sum(a * a, axis=1, keepdims=True)
    scale = lax.rsqrt(squares / D + EPS)
    wide = jnp.concatenate([got[k] for k in range(8)], axis=1)
    hidden = []
    for i in range(4):
        pre = jnp.dot(wide, up[:, 256 * i : 256 * i + 256], preferred_element_type=F32) * scale
        act = 0.5 * pre * (1.0 + jnp.tanh(GELU * (pre + 0.044715 * (pre * pre * pre))))
        hidden.append(act.astype(BF))
    hidden = jnp.concatenate(hidden, axis=1)
    decoded = jnp.dot(resid[...].astype(BF), own_dec[...], preferred_element_type=F32)
    for z in range(8):
        at = slice(256 * z, 256 * z + 256)
        part = jnp.dot(hidden, down[:, at], preferred_element_type=F32).astype(BF)
        out[z, :, 0:256] = part
        for i in range(2):
            side = slice(128 * i, 128 * i + 128)
            decoded += jnp.dot(part[:, side], shared[z, 0:128, side], preferred_element_type=F32)
    decoded = decoded.astype(BF)
    for z in range(8):
        out[z, :, 256:384] = decoded


def final_kernel(got, resid, normal, own_dec, state, guidance):
    total = resid[...]
    decoded = jnp.zeros((128, 128), F32)
    for k in range(8):
        total += got[k, :, 0:256].astype(F32)
        decoded += got[k, :, 256:384].astype(F32)
    state[...] = total.astype(BF)
    grad = normal[:, 0:128] * decoded - normal[:, 640:768]
    for i, d in enumerate(STEPS):
        if i:
            a = normal[:, 128 * i : 128 * i + 128]
            grad += a * pltpu.roll(decoded, 128 - d, 1) + pltpu.roll(a * decoded, d, 1)
    guidance[...] = lax.dot_general(
        grad,
        own_dec[...].astype(F32),
        NT,
        precision=lax.Precision.HIGHEST,
        preferred_element_type=F32,
    )


def stay(x):
    return pltpu.with_memory_space_constraint(x, pltpu.HBM)


def sds(shape, dtype=BF):
    return jax.ShapeDtypeStruct(shape, dtype)


def body(
    states,
    w_qkv,
    w_out,
    w_up,
    w_down,
    w_dec,
    gain_attn,
    gain_mlp,
    obs_patch,
    obs_base,
    obs_count,
    obs_weight,
    obs_value,
):
    n_tok, n_mlp = 32, 8
    x = states.reshape(128, 256)
    me = lax.axis_index("mlp").astype(jnp.int32).reshape(1)
    core = lax.rem(lax.axis_index("tok"), 2).astype(jnp.int32).reshape(1)
    pairs = [(i, i ^ 1) for i in range(n_tok)]
    chips = [[2 * i + c for i in range(16)] for c in range(2)]
    order = (4, 3, 5, 2, 6, 1, 7)
    ring = [[(i, (i + d) % n_mlp) for i in range(n_mlp)] for d in range(n_mlp)]
    vmem = pl.BlockSpec(memory_space=pltpu.VMEM)
    hbm = pl.BlockSpec(memory_space=pltpu.HBM)
    smem = pl.BlockSpec(memory_space=pltpu.SMEM)
    whole = lambda *shape: pl.BlockSpec(shape, lambda i: (0,) * len(shape))

    other = lax.ppermute(x, "tok", pairs)
    send, both, far = pl.pallas_call(
        pack_kernel,
        in_specs=[smem] + [hbm] * 10 + [vmem],
        out_specs=(hbm, hbm, hbm),
        out_shape=(
            pltpu.HBM((32, 272, 128), BF),
            pltpu.HBM((416, 256), BF),
            pltpu.HBM((208, 256), BF),
        ),
        scratch_shapes=[
            pltpu.VMEM((64, 768), BF),
            pltpu.VMEM((64, 256), BF),
            pltpu.VMEM((1, 32, 64), jnp.int32),
            pltpu.VMEM((1, 32, 64), jnp.int32),
            pltpu.VMEM((1, 32, 4, 64), F32),
            pltpu.VMEM((1, 32, 64), F32),
            pltpu.VMEM((2, 256, 128), BF),
            pltpu.VMEM((32, 16, 128), BF),
            pltpu.SMEM((1, 32), jnp.int32),
            pltpu.VMEM((256, 128), BF),
            pltpu.VMEM((1, 256), F32),
            pltpu.VMEM((416, 256), BF),
            pltpu.VMEM((208, 256), BF),
            pltpu.SemaphoreType.DMA((47,)),
        ],
        compiler_params=params(8),
    )(
        core,
        *map(stay, (w_qkv, w_out.T, obs_patch, obs_base, obs_weight, obs_value, obs_count)),
        stay(w_dec),
        stay(gain_mlp.reshape(1, 256)),
        stay(x),
        other,
    )


    def shifted(k):
        return [
            (t * n_mlp + z, t * n_mlp + (z + (k if t % 2 == 0 else -k)) % n_mlp)
            for t in range(n_tok)
            for z in range(n_mlp)
        ]

    def gathered(near, far):
        mine = [lax.ppermute(near, ("tok", "mlp"), shifted(k)) for k in (1, 2, 3)]
        far_in = lax.ppermute(far, "mlp", ring[4])
        theirs = [lax.ppermute(r, "tok", pairs) for r in mine]
        return far_in, mine, theirs

    weights_in = lax.all_to_all(send, "tok", 0, 0, tiled=True)
    far_in, mine, theirs = gathered(both, far)
    packs = (both, far_in, lax.ppermute(far_in, "tok", pairs), *mine, *theirs)
    normed = pl.pallas_call(
        norm_kernel,
        in_specs=[smem] * 2 + [hbm] * 9 + [vmem],
        out_shape=sds((8, 256, 256)),
        scratch_shapes=[pltpu.VMEM((8, 256, 256), BF), pltpu.SemaphoreType.DMA((13,))],
        compiler_params=params(8),
    )(
        me,
        core,
        *map(stay, packs),
        gain_attn.reshape(8, 1, 256),
    )
    qkv, slots = pl.pallas_call(
        qkv_kernel,
        out_shape=(sds((16, 48, 128)), sds((64, 256))),
        compiler_params=params(8),
    )(normed, weights_in)
    qkv_in = lax.all_to_all(qkv, "tok", 0, 0, tiled=True, axis_index_groups=chips)
    half_out, _ = lax.optimization_barrier((weights_in, qkv))
    half_out = lax.ppermute(half_out[:, 192:256, :], "tok", pairs)

    attended = pl.pallas_call(
        attend_kernel,
        in_specs=[smem, vmem],
        out_shape=sds((16, 2, 16, 128)),
        compiler_params=params(8),
    )(core, qkv_in)
    back = lax.all_to_all(attended.reshape(32, 16, 128), "tok", 0, 0, tiled=True)
    back, half_out = lax.optimization_barrier((back, half_out))

    shares = pl.pallas_call(
        share_kernel,
        grid=(1,),
        in_specs=[
            smem,
            smem,
            whole(8, 2, 2, 16, 128),
            pl.BlockSpec((32, 64, 128), lambda i: (0, 3, 0)),
            whole(32, 64, 128),
            whole(64, 256),
        ],
        out_specs=[whole(192, 256)] * 8,
        out_shape=[sds((192, 256))] * 8,
        scratch_shapes=[pltpu.VMEM((8, 128, 256), BF)],
        compiler_params=params(8),
    )(me, core, back.reshape(8, 2, 2, 16, 128), weights_in, half_out, slots)
    shares_in = [shares[0]] + [lax.ppermute(shares[d], "mlp", ring[d]) for d in order]

    resid, scaled, slots_in = pl.pallas_call(
        resid_kernel,
        out_shape=(sds((128, 256), F32), sds((8, 128, 256)), sds((8, 64, 256))),
        compiler_params=params(8),
    )(x, gain_mlp.reshape(1, 256), *shares_in)
    wide = lax.all_to_all(scaled, "mlp", 0, 0, tiled=True)

    down_out = pl.pallas_call(
        ffn_kernel,
        in_specs=[smem] * 2 + [vmem] + [hbm] * 9 + [vmem] * 4,
        out_shape=sds((8, 128, 384)),
        scratch_shapes=[
            pltpu.VMEM((8, 160, 256), BF),
            pltpu.SemaphoreType.DMA((9,)),
        ],
        compiler_params=params(8),
    )(
        me,
        core,
        wide,
        *map(stay, packs),
        w_up,
        w_down,
        resid,
        w_dec,
    )
    down_in = lax.all_to_all(down_out, "mlp", 0, 0, tiled=True)

    slots, _ = lax.optimization_barrier((slots_in, down_out))
    normal = pl.pallas_call(
        normal_kernel,
        grid=(1,),
        in_specs=[whole(8, 64, 256)],
        out_specs=whole(128, 768),
        out_shape=sds((128, 768), F32),
        scratch_shapes=[pltpu.VMEM((128, 512), BF)] * 2 + [pltpu.VMEM((768, 512), BF)] * 2,
        compiler_params=params(8),
        cost_estimate=pl.CostEstimate(
            flops=4_000_000_000, bytes_accessed=1_000_000, transcendentals=0
        ),
    )(slots)
    down_in, normal = lax.optimization_barrier((down_in, normal))

    state, guidance = pl.pallas_call(
        final_kernel,
        out_shape=(sds((128, 256)), sds((128, 256), F32)),
        compiler_params=params(8),
    )(down_in, resid, normal, w_dec)
    return state.reshape(8, 16, 256), guidance.reshape(8, 16, 256)


def solution(mesh):
    placed = (
        P(None, "tok", "mlp"),
        P("tok", "mlp"),
        P("mlp", "tok"),
        P(None, "mlp"),
        P("mlp", None),
        P("mlp", None),
        P(),
        P("mlp"),
        P(("tok", "mlp"), None, None),
        P(("tok", "mlp"), None, None),
        P(("tok", "mlp"), None),
        P(("tok", "mlp"), None, None, None),
        P(("tok", "mlp"), None, None),
    )
    return jax.shard_map(
        body,
        mesh=mesh,
        in_specs=placed,
        out_specs=(P(None, "tok", "mlp"), P(None, "tok", "mlp")),
        check_vma=False,
    )
```

```python
import functools

import jax
import jax.numpy as jnp
from jax import lax
from jax.experimental import pallas as pl
from jax.experimental.pallas import tpu as pltpu
from jax.sharding import PartitionSpec as P

D = 2048
HD = 64
EPS = 1e-06
BF = jnp.bfloat16
F32 = jnp.float32
NT = (((1,), (1,)), ((), ()))
GELU = 0.7978845608028654
STEPS = (0, 1, 15, 16, 17)


def params(mib):
    return pltpu.CompilerParams(vmem_limit_bytes=mib * 1024 * 1024)


def lanes(shape):
    return lax.broadcasted_iota(jnp.int32, shape, len(shape) - 1)


def half(x):
    return pltpu.roll(x, 64, 1)


def left(shape):
    return lanes(shape) < 64


def fetch(pairs, sem):
    copies = [pltpu.make_async_copy(src, dst, sem.at[i]) for i, (src, dst) in enumerate(pairs)]
    for copy in copies:
        copy.start()
    for copy in copies:
        copy.wait()


def pack_kernel(core, *refs):
    ins, (out, both, far), bufs = refs[:11], refs[11:14], refs[14:22]
    counts, w_buf, g_buf, both_buf, far_buf, sem = refs[22:]
    wqkv, wout_t, patch, base, weight, value, blocks, obs = bufs
    dests = [*bufs[:6], counts, w_buf, g_buf]
    dests += [both_buf.at[pl.ds(0, 128), :]]
    loads = [pltpu.make_async_copy(ins[i], dests[i], sem.at[i]) for i in range(10)]
    loads.append(pltpu.make_async_copy(ins[9], far_buf.at[pl.ds(0, 128), :], sem.at[10]))
    for load in loads:
        load.start()
    loads[0].wait()
    loads[1].wait()
    for c in range(2):
        for j in range(3):
            blocks[c, 64 * j : 64 * j + 64, :] = wqkv[:, 256 * j + 128 * c : 256 * j + 128 * c + 128]
        blocks[c, 192:256, :] = wout_t[:, 128 * c : 128 * c + 128]
    n = out.shape[0]
    copies = [
        pltpu.make_async_copy(blocks.at[d % 2], out.at[d, pl.ds(0, 256), :], sem.at[12 + d])
        for d in range(n)
    ]
    for copy in copies:
        copy.start()
    for load in loads[2:]:
        load.wait()
    g = g_buf[...]
    high = g.astype(BF).astype(F32)
    mid = (g - high).astype(BF).astype(F32)
    rows = jnp.concatenate([high, mid, g - high - mid, jnp.zeros((13, 256), F32)], axis=0)
    both_buf[128:256, :] = ins[10][...]
    both_buf[256:384, 0:128] = w_buf[0:128, :]
    both_buf[256:384, 128:256] = w_buf[128:256, :]
    both_buf[384:400, :] = rows.astype(BF)
    both_buf[400:416, :] = jnp.zeros((16, 256), BF)
    far_buf[128:208, :] = both_buf[pl.ds(pl.multiple_of(256 + 80 * core[0], 16), 80), :]
    more = [
        pltpu.make_async_copy(both_buf, both, sem.at[13 + n]),
        pltpu.make_async_copy(far_buf, far, sem.at[14 + n]),
    ]
    for copy in more:
        copy.start()
    copies += more
    slots = lanes((4, 64))
    zero = jnp.zeros((1, 64), F32)
    rest = jnp.zeros((12, 128), F32)
    for dest in range(n):
        row = slice(dest, dest + 1)
        live = slots < counts[0, dest]
        w = jnp.where(live, weight[0, dest], 0.0)
        v = jnp.where(live[0:1], value[0, row, :], 0.0)
        other = [v, patch[0, row, :].astype(F32), base[0, row, :].astype(F32), zero]
        both = jnp.concatenate([w, jnp.concatenate(other, axis=0)], axis=1)
        obs[dest] = jnp.concatenate([both, rest], axis=0).astype(BF)
    last = pltpu.make_async_copy(obs, out.at[:, pl.ds(256, 16), :], sem.at[12 + n])
    last.start()
    for copy in copies:
        copy.wait()
    last.wait()


def groups_of(me, core):
    turn = 1 - 2 * core[0]
    mine = [lax.rem(me[0] - turn * k + 8, 8) for k in (1, 2, 3)]
    theirs = [lax.rem(me[0] + turn * k + 8, 8) for k in (1, 2, 3)]
    return mine, theirs, lax.rem(me[0] + 4, 8)


def norm_kernel(me, core, *refs):
    both, far, far_sib, mine, theirs = *refs[:3], refs[3:6], refs[6:9]
    gain, out, buf, sem = refs[9:]
    near, across, opposite = groups_of(me, core)
    low, top = pl.ds(0, 128), pl.ds(128, 128)
    pairs = [
        (both.at[pl.ds(0, 256), :], buf.at[me[0]]),
        (far.at[low, :], buf.at[opposite, low, :]),
        (far_sib.at[low, :], buf.at[opposite, top, :]),
    ]
    for k in range(3):
        pairs.append((mine[k].at[pl.ds(0, 256), :], buf.at[near[k]]))
        pairs.append((theirs[k].at[top, :], buf.at[across[k], low, :]))
        pairs.append((theirs[k].at[low, :], buf.at[across[k], top, :]))
    fetch(pairs, sem)
    squares = jnp.zeros((256, 1), F32)
    for k in range(8):
        a = buf[k].astype(F32)
        squares += jnp.sum(a * a, axis=1, keepdims=True)
    r = lax.rsqrt(squares / D + EPS)
    for k in range(8):
        out[k] = (buf[k].astype(F32) * r * gain[k]).astype(BF)


def qkv_kernel(normed, w, out, slots):
    acc = jnp.zeros((256, 384), F32)
    for k in range(8):
        cols = [w[4 * k : 4 * k + 4, 64 * j : 64 * j + 64, :].reshape(256, 128) for j in range(3)]
        acc += jnp.dot(normed[k], jnp.concatenate(cols, axis=1), preferred_element_type=F32)
    q, k, v = acc[:, 0:128], acc[:, 128:256], acc[:, 256:384]
    low = left((256, 128))
    pairs = (jnp.where(low, q, half(k)), jnp.where(low, half(q), k))
    own, sib = v[0:128], v[128:256]
    low = left((128, 128))
    values = (jnp.where(low, own, half(sib)), jnp.where(low, half(own), sib))
    for g in range(2):
        qk = pairs[g].astype(BF)
        vv = values[g].astype(BF)
        for s in range(8):
            out[2 * s + g, 0:16, :] = qk[16 * s : 16 * s + 16, :]
            out[2 * s + g, 16:32, :] = qk[128 + 16 * s : 144 + 16 * s, :]
            out[2 * s + g, 32:48, :] = vv[16 * s : 16 * s + 16, :]
    low = left((16, 128))
    tiles = []
    for pair in range(16):
        a = w[2 * pair, 256:272, :].astype(F32)
        b = w[2 * pair + 1, 256:272, :].astype(F32)
        tiles.append(jnp.where(low, a, half(b))[0:4])
        tiles.append(jnp.where(low, half(a), b)[0:4])
    slots[:, 0:128] = jnp.concatenate(tiles[:16], axis=0).astype(BF)
    slots[:, 128:256] = jnp.concatenate(tiles[16:], axis=0).astype(BF)


def attend_kernel(core, got, out):
    qk_own = got[:, 0:16, :].reshape(256, 128)
    qk_sib = got[:, 16:32, :].reshape(256, 128)
    vv = got[:, 32:48, :].reshape(256, 128)
    low = left((256, 128))

    def mix(qk):
        query = (jnp.where(low, 0.0, half(qk.astype(F32))) * (1.0 / HD**0.5)).astype(BF)
        first = lax.dot_general(query, qk_own, NT, preferred_element_type=F32)
        second = lax.dot_general(query, qk_sib, NT, preferred_element_type=F32)
        top = jnp.maximum(
            jnp.max(first, axis=1, keepdims=True), jnp.max(second, axis=1, keepdims=True)
        )
        first = jnp.exp(first - top)
        second = jnp.exp(second - top)
        total = jnp.sum(first, axis=1, keepdims=True) + jnp.sum(second, axis=1, keepdims=True)
        one = jnp.dot(first.astype(BF), vv, preferred_element_type=F32)
        two = jnp.dot(second.astype(BF), vv, preferred_element_type=F32)
        return (one + half(two)) / total

    c = core[0]
    out[:, c] = mix(qk_own).astype(BF).reshape(16, 16, 128)
    out[:, 1 - c] = mix(qk_sib).astype(BF).reshape(16, 16, 128)


def share_kernel(me, core, got, w, w_sib, slots, *refs):
    outs, buf = refs[:8], refs[8]
    low = left((128, 128))

    def heads_of(c):
        a = got[:, 0, c].reshape(128, 128).astype(F32)
        b = got[:, 1, c].reshape(128, 128).astype(F32)
        return jnp.where(low, a, half(b)).astype(BF)

    own, other = heads_of(core[0]), heads_of(1 - core[0])
    for z in range(8):
        at = slice(4 * z, 4 * z + 4)
        part = lax.dot_general(own, w[at].reshape(256, 128), NT, preferred_element_type=F32)
        part += lax.dot_general(other, w_sib[at].reshape(256, 128), NT, preferred_element_type=F32)
        buf[z] = part.astype(BF)
    for d in range(8):
        outs[d][0:128, :] = buf[lax.rem(me[0] + d, 8)]
        outs[d][128:192, :] = slots[...]


def normal_kernel(slots, out, hot_a, hot_b, terms_a, terms_b):
    cells = lax.broadcasted_iota(jnp.int32, (128, 128), 0).astype(F32).astype(BF)
    zero = jnp.zeros((128, 128), BF)
    one = jnp.ones((128, 128), BF)

    def place(*picks):
        out = zero
        for e, x in picks:
            out = jnp.where(e, jnp.broadcast_to(x.astype(BF), (128, 128)), out)
        return out

    def build(step, hot, terms):
        group, first = lax.div(step, 4), lax.rem(step, 2) * 32
        side = pl.ds(pl.multiple_of(lax.div(lax.rem(step, 4), 2) * 128, 128), 128)
        for c in range(2):
            rows = slots[group, pl.ds(pl.multiple_of(first + 16 * c, 16), 16), side].astype(F32)
            for h in range(2):
                t = rows[8 * h : 8 * h + 8]
                w0, w1, w2, w3, v = (t[j : j + 1] for j in range(5))
                rel = cells - jnp.broadcast_to(t[6:7].astype(BF), (128, 128))
                e0, e1, e2, e3 = rel == 0, rel == 1, rel == 16, rel == 17
                parts = (
                    place((e0, w0 * w0), (e1, w1 * w1), (e2, w2 * w2), (e3, w3 * w3)),
                    place((e0, w0 * w1), (e2, w2 * w3)),
                    place((e1, w1 * w2)),
                    place((e0, w0 * w2), (e1, w1 * w3)),
                    place((e0, w0 * w3)),
                    place((e0, v * w0), (e1, v * w1), (e2, v * w2), (e3, v * w3)),
                )
                at = slice(256 * c + 128 * h, 256 * c + 128 * h + 128)
                patch = jnp.broadcast_to(t[5:6].astype(BF), (128, 128))
                hot[:, at] = jnp.where(cells == patch, one, zero)
                for j, part in enumerate(parts):
                    terms[128 * j : 128 * j + 128, at] = part

    def add(hot, terms):
        out[...] += lax.dot_general(hot[...], terms[...], NT, preferred_element_type=F32)

    out[...] = jnp.zeros(out.shape, F32)
    build(jnp.int32(0), hot_a, terms_a)

    def two(i, _):
        add(hot_a, terms_a)
        build(2 * i + 1, hot_b, terms_b)
        add(hot_b, terms_b)
        build(2 * i + 2, hot_a, terms_a)
        return 0

    lax.fori_loop(0, 15, two, 0)
    add(hot_a, terms_a)
    build(jnp.int32(31), hot_b, terms_b)
    add(hot_b, terms_b)


def resid_kernel(x, gain, *refs):
    got, (resid, scaled, slots) = refs[:8], refs[8:]
    total = x[...].astype(F32)
    for d in range(8):
        total += got[d][0:128, :].astype(F32)
        slots[d] = got[d][128:192, :]
    resid[...] = total
    scaled[...] = (total * gain[...]).astype(BF)


def ffn_kernel(me, core, *refs):
    blocks, refs = refs[:8], refs[8:]
    own, far, far_sib, mine, theirs = refs[0], refs[1], refs[2], refs[3:6], refs[6:9]
    up, down, resid, own_dec, out, shared, got, sem = refs[9:]
    for d in range(8):
        got[lax.rem(me[0] - d + 8, 8)] = blocks[d][...]
    near, across, opposite = groups_of(me, core)
    common = pl.ds(256, 160)
    pairs = [(own.at[common, :], shared.at[me[0]])]
    for half_far, c in ((far, core[0]), (far_sib, 1 - core[0])):
        side = pl.ds(pl.multiple_of(80 * c, 16), 80)
        pairs.append((half_far.at[pl.ds(128, 80), :], shared.at[opposite, side, :]))
    for k in range(3):
        pairs.append((mine[k].at[common, :], shared.at[near[k]]))
        pairs.append((theirs[k].at[common, :], shared.at[across[k]]))
    fetch(pairs, sem)
    squares = jnp.zeros((128, 1), F32)
    for k in range(8):
        g = shared[k, 128:144, :].astype(F32)
        a = got[k].astype(F32) / (g[0:1] + g[1:2] + g[2:3])
        squares += jnp.sum(a * a, axis=1, keepdims=True)
    scale = lax.rsqrt(squares / D + EPS)
    wide = jnp.concatenate([got[k] for k in range(8)], axis=1)
    hidden = []
    for i in range(4):
        pre = jnp.dot(wide, up[:, 256 * i : 256 * i + 256], preferred_element_type=F32) * scale
        act = 0.5 * pre * (1.0 + jnp.tanh(GELU * (pre + 0.044715 * (pre * pre * pre))))
        hidden.append(act.astype(BF))
    hidden = jnp.concatenate(hidden, axis=1)
    decoded = jnp.dot(resid[...].astype(BF), own_dec[...], preferred_element_type=F32)
    for z in range(8):
        at = slice(256 * z, 256 * z + 256)
        part = jnp.dot(hidden, down[:, at], preferred_element_type=F32).astype(BF)
        out[z, :, 0:256] = part
        for i in range(2):
            side = slice(128 * i, 128 * i + 128)
            decoded += jnp.dot(part[:, side], shared[z, 0:128, side], preferred_element_type=F32)
    decoded = decoded.astype(BF)
    for z in range(8):
        out[z, :, 256:384] = decoded


def final_kernel(got, resid, normal, own_dec, state, guidance):
    total = resid[...]
    decoded = jnp.zeros((128, 128), F32)
    for k in range(8):
        total += got[k, :, 0:256].astype(F32)
        decoded += got[k, :, 256:384].astype(F32)
    state[...] = total.astype(BF)
    grad = normal[:, 0:128] * decoded - normal[:, 640:768]
    for i, d in enumerate(STEPS):
        if i:
            a = normal[:, 128 * i : 128 * i + 128]
            grad += a * pltpu.roll(decoded, 128 - d, 1) + pltpu.roll(a * decoded, d, 1)
    guidance[...] = lax.dot_general(
        grad,
        own_dec[...].astype(F32),
        NT,
        precision=lax.Precision.HIGHEST,
        preferred_element_type=F32,
    )


def stay(x):
    return pltpu.with_memory_space_constraint(x, pltpu.HBM)


def sds(shape, dtype=BF):
    return jax.ShapeDtypeStruct(shape, dtype)


def body(
    states,
    w_qkv,
    w_out,
    w_up,
    w_down,
    w_dec,
    gain_attn,
    gain_mlp,
    obs_patch,
    obs_base,
    obs_count,
    obs_weight,
    obs_value,
):
    n_tok, n_mlp = 32, 8
    x = states.reshape(128, 256)
    me = lax.axis_index("mlp").astype(jnp.int32).reshape(1)
    core = lax.rem(lax.axis_index("tok"), 2).astype(jnp.int32).reshape(1)
    pairs = [(i, i ^ 1) for i in range(n_tok)]
    chips = [[2 * i + c for i in range(16)] for c in range(2)]
    order = (4, 3, 5, 2, 6, 1, 7)
    ring = [[(i, (i + d) % n_mlp) for i in range(n_mlp)] for d in range(n_mlp)]
    vmem = pl.BlockSpec(memory_space=pltpu.VMEM)
    hbm = pl.BlockSpec(memory_space=pltpu.HBM)
    smem = pl.BlockSpec(memory_space=pltpu.SMEM)
    whole = lambda *shape: pl.BlockSpec(shape, lambda i: (0,) * len(shape))

    other = lax.ppermute(x, "tok", pairs)
    send, both, far = pl.pallas_call(
        pack_kernel,
        in_specs=[smem] + [hbm] * 10 + [vmem],
        out_specs=(hbm, hbm, hbm),
        out_shape=(
            pltpu.HBM((32, 272, 128), BF),
            pltpu.HBM((416, 256), BF),
            pltpu.HBM((208, 256), BF),
        ),
        scratch_shapes=[
            pltpu.VMEM((64, 768), BF),
            pltpu.VMEM((64, 256), BF),
            pltpu.VMEM((1, 32, 64), jnp.int32),
            pltpu.VMEM((1, 32, 64), jnp.int32),
            pltpu.VMEM((1, 32, 4, 64), F32),
            pltpu.VMEM((1, 32, 64), F32),
            pltpu.VMEM((2, 256, 128), BF),
            pltpu.VMEM((32, 16, 128), BF),
            pltpu.SMEM((1, 32), jnp.int32),
            pltpu.VMEM((256, 128), BF),
            pltpu.VMEM((1, 256), F32),
            pltpu.VMEM((416, 256), BF),
            pltpu.VMEM((208, 256), BF),
            pltpu.SemaphoreType.DMA((47,)),
        ],
        compiler_params=params(8),
    )(
        core,
        *map(stay, (w_qkv, w_out.T, obs_patch, obs_base, obs_weight, obs_value, obs_count)),
        stay(w_dec),
        stay(gain_mlp.reshape(1, 256)),
        stay(x),
        other,
    )


    def shifted(k):
        return [
            (t * n_mlp + z, t * n_mlp + (z + (k if t % 2 == 0 else -k)) % n_mlp)
            for t in range(n_tok)
            for z in range(n_mlp)
        ]

    def gathered(near, far):
        mine = [lax.ppermute(near, ("tok", "mlp"), shifted(k)) for k in (1, 2, 3)]
        far_in = lax.ppermute(far, "mlp", ring[4])
        theirs = [lax.ppermute(r, "tok", pairs) for r in mine]
        return far_in, mine, theirs

    weights_in = lax.all_to_all(send, "tok", 0, 0, tiled=True)
    far_in, mine, theirs = gathered(both, far)
    packs = (both, far_in, lax.ppermute(far_in, "tok", pairs), *mine, *theirs)
    normed = pl.pallas_call(
        norm_kernel,
        in_specs=[smem] * 2 + [hbm] * 9 + [vmem],
        out_shape=sds((8, 256, 256)),
        scratch_shapes=[pltpu.VMEM((8, 256, 256), BF), pltpu.SemaphoreType.DMA((13,))],
        compiler_params=params(8),
    )(
        me,
        core,
        *map(stay, packs),
        gain_attn.reshape(8, 1, 256),
    )
    qkv, slots = pl.pallas_call(
        qkv_kernel,
        out_shape=(sds((16, 48, 128)), sds((64, 256))),
        compiler_params=params(8),
    )(normed, weights_in)
    qkv_in = lax.all_to_all(qkv, "tok", 0, 0, tiled=True, axis_index_groups=chips)
    half_out, _ = lax.optimization_barrier((weights_in, qkv))
    half_out = lax.ppermute(half_out[:, 192:256, :], "tok", pairs)

    attended = pl.pallas_call(
        attend_kernel,
        in_specs=[smem, vmem],
        out_shape=sds((16, 2, 16, 128)),
        compiler_params=params(8),
    )(core, qkv_in)
    back = lax.all_to_all(attended.reshape(32, 16, 128), "tok", 0, 0, tiled=True)
    back, half_out = lax.optimization_barrier((back, half_out))

    shares = pl.pallas_call(
        share_kernel,
        grid=(1,),
        in_specs=[
            smem,
            smem,
            whole(8, 2, 2, 16, 128),
            pl.BlockSpec((32, 64, 128), lambda i: (0, 3, 0)),
            whole(32, 64, 128),
            whole(64, 256),
        ],
        out_specs=[whole(192, 256)] * 8,
        out_shape=[sds((192, 256))] * 8,
        scratch_shapes=[pltpu.VMEM((8, 128, 256), BF)],
        compiler_params=params(8),
    )(me, core, back.reshape(8, 2, 2, 16, 128), weights_in, half_out, slots)
    shares_in = [shares[0]] + [lax.ppermute(shares[d], "mlp", ring[d]) for d in order]

    resid, scaled, slots_in = pl.pallas_call(
        resid_kernel,
        out_shape=(sds((128, 256), F32), sds((128, 256)), sds((8, 64, 256))),
        compiler_params=params(8),
    )(x, gain_mlp.reshape(1, 256), *shares_in)
    wide = {d: lax.ppermute(scaled, "mlp", ring[d]) for d in order}
    wide[0] = scaled

    down_out = pl.pallas_call(
        ffn_kernel,
        in_specs=[smem] * 2 + [vmem] * 8 + [hbm] * 9 + [vmem] * 4,
        out_shape=sds((8, 128, 384)),
        scratch_shapes=[
            pltpu.VMEM((8, 160, 256), BF),
            pltpu.VMEM((8, 128, 256), BF),
            pltpu.SemaphoreType.DMA((9,)),
        ],
        compiler_params=params(8),
    )(
        me,
        core,
        *[wide[d] for d in range(8)],
        *map(stay, packs),
        w_up,
        w_down,
        resid,
        w_dec,
    )
    down_in = lax.all_to_all(down_out, "mlp", 0, 0, tiled=True)

    slots, _ = lax.optimization_barrier((slots_in, down_out))
    normal = pl.pallas_call(
        normal_kernel,
        grid=(1,),
        in_specs=[whole(8, 64, 256)],
        out_specs=whole(128, 768),
        out_shape=sds((128, 768), F32),
        scratch_shapes=[pltpu.VMEM((128, 512), BF)] * 2 + [pltpu.VMEM((768, 512), BF)] * 2,
        compiler_params=params(8),
        cost_estimate=pl.CostEstimate(
            flops=4_000_000_000, bytes_accessed=1_000_000, transcendentals=0
        ),
    )(slots)
    down_in, normal = lax.optimization_barrier((down_in, normal))

    state, guidance = pl.pallas_call(
        final_kernel,
        out_shape=(sds((128, 256)), sds((128, 256), F32)),
        compiler_params=params(8),
    )(down_in, resid, normal, w_dec)
    return state.reshape(8, 16, 256), guidance.reshape(8, 16, 256)


def solution(mesh):
    placed = (
        P(None, "tok", "mlp"),
        P("tok", "mlp"),
        P("mlp", "tok"),
        P(None, "mlp"),
        P("mlp", None),
        P("mlp", None),
        P(),
        P("mlp"),
        P(("tok", "mlp"), None, None),
        P(("tok", "mlp"), None, None),
        P(("tok", "mlp"), None),
        P(("tok", "mlp"), None, None, None),
        P(("tok", "mlp"), None, None),
    )
    return jax.shard_map(
        body,
        mesh=mesh,
        in_specs=placed,
        out_specs=(P(None, "tok", "mlp"), P(None, "tok", "mlp")),
        check_vma=False,
    )
```
